32 devices in a mesh: groups: 2 (over x), tile: 8 (over z, y), example: 2 (over core).
Axes of the slice: x: 2, y: 2, z: 4, core: 2. Of those that a mesh axis runs over, the one named last changes fastest.
Arguments:
- features: bfloat16 [4096, 8192], P(('groups', 'example'), 'tile'), parts along dimension 0
- tile_lists: int32 [272, 3], P('groups'), parts along dimension 0, may hold values from 0 to 15, as said below
- noise_tiles: float32 [544, 512, 512], P(('groups', 'tile'), 'example'), parts along dimension 0, may hold values from -6 to 6
Outputs:
- covariance: float32 [544, 512, 512], P(('groups', 'tile'), 'example'), parts along dimension 0
The draws below stay inside these ranges and needn't reach their ends.
There are 2 independent parts, one for each index of `groups`. The reference program is written for one: setup_inputs(seed, part) draws one part's arguments, and reference() takes and returns one part's arrays. A program takes and returns all parts, laid end to end along the dimension named above; each array names one. Nothing has to cross between parts.
Inputs may be any that keep to these rules, and one draw needn't show every extreme that they name: `tile_lists`: every tile (i, j) with 0 <= j <= i < 16 appears once, in an order drawn from the seed; owners lie in 0 to 7, no owner has more than 34 tiles and some owner has exactly 34.
All inputs are finite; a program needn't handle non-finite values.
Results may differ from the reference program's by a relative error of at most 0.0023.
Values may be sent and summed in bfloat16 or wider, within the bound.
No kernel may reach another device: no remote copies, remote signals or barrier semaphores. Data moves between devices by JAX's collectives and lax.ppermute only.
A program may use at most 192 MiB of HBM per device.

```python
import math
import jax
import jax.numpy as jnp
from jax import lax

F = 8192
STRIPE = 512
ROWS = 2048
NS = 16
TILES = 136
SLOTS = 34
OWNED = 272
N_TILE = 8


def draw_features(key, part):
    key = jax.random.fold_in(key, 5)
    key_base, key_rows = jax.random.split(key, 2)
    row_scale = jnp.exp(jax.random.uniform(key_rows, (ROWS, 1), jnp.float32, math.log(0.3), math.log(3.0)))
    column_scale = jnp.sqrt(1.0 + 2.0 * jnp.arange(F, dtype=jnp.float32) / F)[None, :]
    base = jax.random.normal(key_base, (ROWS, F), jnp.float32)
    return jnp.clip(base * row_scale * column_scale, -16.0, 16.0).astype(jnp.bfloat16)


def draw_tile_lists(key, part):
    key = jax.random.fold_in(key, 11)
    key_full, key_weight, key_score, key_order = jax.random.split(key, 4)
    total = N_TILE * SLOTS
    position = jnp.arange(total, dtype=jnp.int32)
    owner_of = position // SLOTS
    slot_of = position % SLOTS
    full_owner = jax.random.randint(key_full, (), 0, N_TILE)
    owner_weight = jax.random.randint(key_weight, (N_TILE,), 0, 4)
    jitter = jax.random.randint(key_score, (total,), 0, 65536)
    score = owner_weight[owner_of] * 65536 + jitter
    score = score + jnp.where(owner_of == full_owner, 1048576, 0)
    score = score + jnp.where((owner_of == N_TILE - 1) & (slot_of == 0), 1048576, 0)
    score = score * total + position
    _, chosen = lax.top_k(score, TILES)
    owners = (chosen // SLOTS).astype(jnp.int32)
    tile_ids = jax.random.permutation(key_order, TILES).astype(jnp.int32)
    levels = jnp.arange(1, NS, dtype=jnp.int32)
    bases = levels * (levels + 1) // 2
    first = jnp.sum((bases[None, :] <= tile_ids[:, None]).astype(jnp.int32), axis=1)
    second = tile_ids - first * (first + 1) // 2
    return jnp.stack([first, second, owners], axis=1).astype(jnp.int32)


def steps_of(own_key, dims, cuts, low, high):
    gain = 1.0
    for dim, parts in cuts:
        draws = jax.random.uniform(jax.random.fold_in(jax.random.fold_in(own_key, 6), dim), (parts,), jnp.float32, low / len(cuts), high / len(cuts))
        gain = gain * jnp.repeat(jnp.exp(draws), dims[dim] // parts).reshape((-1,) + (1,) * (len(dims) - 1 - dim))
    return gain


def normal_values(key, shape, width, most, pieces=(), held_as=jnp.bfloat16):
    drawn = jax.random.normal(key, shape, jnp.float32) * width
    if len(pieces) > 0:
        drawn = steps_of(key, shape, pieces, -0.22, 0.18) * drawn
    return jnp.clip(drawn, min=-most, max=most).astype(held_as)


def setup_inputs(seed: int = 0, part: int = 0) -> dict:
    key_list = jax.random.split(jax.random.key(seed), 4)
    part_keys = jax.random.split(jax.random.fold_in(key_list[3], part), 4)
    features = draw_features(jax.random.fold_in(jax.random.fold_in(key_list[3], part), 71), part)
    tile_lists = draw_tile_lists(jax.random.fold_in(jax.random.fold_in(key_list[3], part), 71), part)
    noise_tiles = normal_values(part_keys[2], (OWNED, STRIPE, STRIPE), 1.0, 6.0, ((0, 8), (1, 2)), jnp.float32)
    return {"features": features, "tile_lists": tile_lists, "noise_tiles": noise_tiles}


def reference(features, tile_lists, noise_tiles):
    values = features.astype(jnp.float32)
    norms = lax.optimization_barrier(jnp.sum(values * values, axis=1, keepdims=True))
    scaled = (values * (1.0 / jnp.maximum(jnp.sqrt(norms), math.sqrt(2.0 * F)))).astype(jnp.bfloat16)
    owners = tile_lists[:, 2]
    position = jnp.arange(TILES, dtype=jnp.int32)
    earlier = (position[None, :] < position[:, None]) & (owners[None, :] == owners[:, None])
    ranks = lax.optimization_barrier(jnp.sum(earlier.astype(jnp.int32), axis=1)).astype(jnp.int32)
    target = (owners * SLOTS + ranks).astype(jnp.int32)
    cov_scale = F / math.sqrt(ROWS)

    def place(result, entry):
        first, second, where_to = entry
        left = lax.dynamic_slice_in_dim(scaled, (first * STRIPE).astype(jnp.int32), STRIPE, 1)
        right = lax.dynamic_slice_in_dim(scaled, (second * STRIPE).astype(jnp.int32), STRIPE, 1)
        gram = jnp.dot(left.T, right, preferred_element_type=jnp.float32)
        block = cov_scale * gram + lax.dynamic_index_in_dim(noise_tiles, where_to, 0, keepdims=False)
        return (lax.dynamic_update_index_in_dim(result, block, where_to, 0), None)
    start = jnp.zeros((OWNED, STRIPE, STRIPE), jnp.float32)
    result, _ = lax.scan(place, start, (tile_lists[:, 0], tile_lists[:, 1], target))
    return result
```

```python
import functools
import math

import jax
import jax.numpy as jnp
import numpy as np
from jax import lax
from jax.experimental import pallas as pl
from jax.experimental.pallas import tpu as pltpu
from jax.sharding import PartitionSpec as P

F = 8192
VMEM = 48 * 1024 * 1024
CORES = [(0, 1), (1, 0)]

Y_SWAP = [(2 * z + y, 2 * z + 1 - y) for z in range(4) for y in range(2)]
Z_SWAP = [(2 * a + y, 2 * b + y) for a, b in ((0, 1), (1, 0), (2, 3), (3, 2)) for y in range(2)]
M_SWAP = [(2 * a + y, 2 * b + y) for a, b in ((1, 2), (2, 1)) for y in range(2)]


def slot_table(tile_lists, owner, slots):
    owners = tile_lists[:, 2]
    entries = tile_lists.shape[0]
    position = jnp.arange(entries, dtype=jnp.int32)
    mine = owners == owner
    earlier = (position[None, :] < position[:, None]) & mine[None, :]
    ranks = jnp.sum(earlier.astype(jnp.int32), axis=1)
    matches = (
        mine[None, :] & (ranks[None, :] == jnp.arange(slots, dtype=jnp.int32)[:, None])
    ).astype(jnp.int32)
    living = jnp.sum(matches, axis=1)
    first = jnp.sum(matches * tile_lists[None, :, 0], axis=1)
    second = jnp.sum(matches * tile_lists[None, :, 1], axis=1)
    return (first, second, living)


def arrivals():
    held = {}
    for z in range(4):
        for y in range(2):
            a = lambda plane, half: 2 * (2 * plane + y) + half
            o = lambda plane, half: 2 * (2 * plane + 1 - y) + half
            if z in (0, 3):
                near = 1 if z == 0 else 2
                over, far = 3 - near, 3 - z
                zs = [a(near, 0), a(near, 1), a(over, 0), a(over, 1), a(far, 0), a(far, 1), o(far, 1)]
                ys = [o(z, 0), o(z, 1), o(near, 0), o(near, 1), o(over, 0), o(over, 1), o(far, 0)]
                ms = [-1] * 4
            else:
                edge = 0 if z == 1 else 3
                over, far = 3 - z, 3 - edge
                zs = [a(edge, 0), a(edge, 1), o(edge, 0), o(edge, 1), -1, -1, -1]
                ys = [o(z, 0), o(z, 1), o(over, 0), o(over, 1), o(far, 0), o(far, 1), -1]
                ms = [a(over, 0), a(over, 1), a(far, 0), a(far, 1)]
            row = {"own0": a(z, 0), "own1": a(z, 1)}
            row.update({f"z{k + 1}": s for k, s in enumerate(zs)})
            row.update({f"y{k + 1}": s for k, s in enumerate(ys)})
            row.update({f"m{k + 1}": s for k, s in enumerate(ms)})
            held[2 * z + y] = row
    return held


STAGES = (
    ("own0", "own1", "z1", "y1", "m1", "z2", "y2", "m2"),
    ("z3", "y3", "m3", "z4", "y4", "m4"),
    ("z5", "y5"),
    ("z6", "y6"),
    ("z7", "y7"),
)


def prep_kernel(meta, mine, other, inv_mine, inv_other, *rest):
    right, left = rest[-2:]
    half = pl.program_id(0)
    width = left.shape[1]
    columns = pl.ds(pl.multiple_of(meta[1] * width, width), width)

    def scale(raw, inv):
        right[0] = (raw[...].astype(jnp.float32) * inv[...]).astype(jnp.bfloat16)
        part = raw[:, columns].astype(jnp.float32) * inv[...]
        left[0] = part.T.astype(jnp.bfloat16)

    @pl.when(half == 0)
    def _():
        scale(mine, inv_mine)

    @pl.when(half == 1)
    def _():
        scale(other, inv_other)


def prepare(meta, mine, other, inv_mine, inv_other, held, after, stripes, height):
    rows, stripe = mine.shape
    chunk = 512
    steps = rows // chunk
    raw = lambda want: pl.BlockSpec(
        (chunk, stripe), lambda h, r, m: (jnp.where(h == want, r, 0 if want else steps - 1), 0)
    )
    inv = lambda want: pl.BlockSpec(
        (chunk, 1), lambda h, r, m: (jnp.where(h == want, r, 0 if want else steps - 1), 0)
    )
    anywhere = pl.BlockSpec(memory_space=pl.ANY)
    extra = [] if held is None else [*held, *after]
    return pl.pallas_call(
        prep_kernel,
        grid_spec=pltpu.PrefetchScalarGridSpec(
            num_scalar_prefetch=1,
            grid=(2, steps),
            in_specs=[raw(0), raw(1), inv(0), inv(1)] + [anywhere] * len(extra),
            out_specs=[
                pl.BlockSpec((1, chunk, stripe), lambda h, r, m: (m[0], h * steps + r, 0)),
                pl.BlockSpec((1, height, chunk), lambda h, r, m: (m[0], 0, h * steps + r)),
            ],
        ),
        out_shape=[
            jax.ShapeDtypeStruct((stripes + 1, 2 * rows, stripe), jnp.bfloat16),
            jax.ShapeDtypeStruct((stripes + 1, height, 2 * rows), jnp.bfloat16),
        ],
        input_output_aliases={} if held is None else {5: 0, 6: 1},
        compiler_params=pltpu.CompilerParams(vmem_limit_bytes=VMEM),
        cost_estimate=pl.CostEstimate(flops=4 * rows * stripe, bytes_accessed=10 * rows * stripe, transcendentals=0),
        name="prepare",
    )(meta, mine, other, inv_mine, inv_other, *extra)


def gram_kernel(cov_scale, stage, lefts, rights, slots, steps, span, left, right, noise, *rest):
    out = rest[-1]
    _, height, stripe = out.shape
    depth = right.shape[1]
    start = span[0]

    def one_tile(l, r, n, o):
        e = start + pl.program_id(0)
        alive = (steps[e] >= 0) & (steps[e] <= stage)

        @pl.when(alive)
        def _():
            gram = jnp.dot(l[0], r[0], preferred_element_type=jnp.float32)
            o[0] = cov_scale * gram + n[0]

        @pl.when(jnp.logical_not(alive))
        def _():
            o[0] = jnp.zeros_like(o[0])

    pltpu.emit_pipeline(
        one_tile,
        grid=(span[1],),
        in_specs=[
            pl.BlockSpec((1, height, depth), lambda e: (lefts[start + e], 0, 0)),
            pl.BlockSpec((1, depth, stripe), lambda e: (rights[start + e], 0, 0)),
            pl.BlockSpec((1, height, stripe), lambda e: (slots[start + e], 0, 0)),
        ],
        out_specs=[pl.BlockSpec((1, height, stripe), lambda e: (slots[start + e], 0, 0))],
    )(left, right, noise, out)


def grams(cov_scale, stage, table, span, right, left, noise, out):
    slots, height, stripe = noise.shape
    depth = right.shape[1]
    extra = [] if out is None else [out]
    anywhere = pl.BlockSpec(memory_space=pl.ANY)
    return pl.pallas_call(
        functools.partial(gram_kernel, cov_scale, stage),
        in_specs=[pl.BlockSpec(memory_space=pltpu.SMEM)] * 5 + [anywhere] * (3 + len(extra)),
        out_specs=anywhere,
        out_shape=jax.ShapeDtypeStruct(noise.shape, jnp.float32),
        input_output_aliases={} if out is None else {8: 0},
        compiler_params=pltpu.CompilerParams(vmem_limit_bytes=VMEM),
        cost_estimate=pl.CostEstimate(
            flops=2 * 8 * height * stripe * depth, bytes_accessed=8 * 4 * 1024 * 1024, transcendentals=0
        ),
        name="grams",
    )(*table, span, left, right, noise, *extra)


def schedule(first, second, living, stage_of, stages):
    slots = first.shape[0]
    look = lambda index: jnp.sum(
        jnp.where(index[:, None] == jnp.arange(stage_of.shape[0])[None, :], stage_of[None, :], 0), axis=1
    )
    stage = jnp.where(living > 0, jnp.maximum(look(first), look(second)), -1)
    position = jnp.arange(slots, dtype=jnp.int32)
    key = (((stage + 1) * 64 + second) * 64 + first) * slots + position
    rank = jnp.sum((key[None, :] < key[:, None]).astype(jnp.int32), axis=1)
    pick = (rank[None, :] == position[:, None]).astype(jnp.int32)
    put = lambda values: jnp.sum(pick * values[None, :], axis=1)
    table = (put(first), put(second), put(position), put(stage))
    spans, begin = [], jnp.int32(0)
    for step in range(stages):
        end = jnp.sum((stage <= step).astype(jnp.int32))
        count = end - begin
        start = jnp.where(count > 0, begin, slots - 1)
        spans.append(jnp.stack([start, jnp.maximum(count, 1)]).astype(jnp.int32))
        begin = end
    return table, spans


def grid_body(features, tile_lists, noise_tiles):
    slots, height, stripe = noise_tiles.shape
    rows = features.shape[0]
    chips = lax.axis_size("tile")
    stripes = features.shape[1] * chips // stripe
    chip = lax.axis_index("tile")
    core = lax.axis_index("example")
    at_end = (chip < 2) | (chip >= chips - 2)
    cov_scale = F / math.sqrt(rows * lax.axis_size("example"))
    y = lambda x: lax.ppermute(x, "tile", Y_SWAP)
    z = lambda x: lax.ppermute(x, "tile", Z_SWAP)
    m = lambda x: lax.ppermute(x, "tile", M_SWAP)
    pick = lambda a, b: jnp.where(at_end, a, b)

    b = {"own0": features[:, :stripe], "own1": features[:, stripe:]}
    for k in (1, 2):
        own = b[f"own{k - 1}"]
        b[f"y{k}"], b[f"z{k}"], b[f"m{k}"] = y(own), z(own), m(own)
    for k in (3, 4):
        near_z, near_m, near_y = b[f"z{k - 2}"], b[f"m{k - 2}"], b[f"y{k - 2}"]
        b[f"y{k}"] = y(pick(near_z, near_m))
        b[f"z{k}"] = z(pick(near_y, near_m))
        b[f"m{k}"] = m(near_z)
    for k in (5, 6):
        near_z, near_m = b[f"z{k - 2}"], b[f"m{k - 2}"]
        b[f"y{k}"] = y(pick(near_z, near_m))
        b[f"z{k}"] = z(near_m)
    b["y7"] = y(b["z5"])
    b["z7"] = z(b["y6"])

    values = features.astype(jnp.float32)
    norms = lax.psum(jnp.sum(values * values, axis=1), "tile")
    inverse = (1.0 / jnp.maximum(jnp.sqrt(norms), math.sqrt(2.0 * F)))[:, None]
    inverse_other = lax.ppermute(inverse, "example", CORES)

    held_at = arrivals()
    stage_of = np.zeros((chips, stripes), np.int32)
    for c in range(chips):
        for s, names in enumerate(STAGES):
            for n in names:
                if held_at[c][n] >= 0:
                    stage_of[c, held_at[c][n]] = s
    first, second, living = slot_table(tile_lists, chip, slots)
    table, spans = schedule(first, second, living, jnp.asarray(stage_of)[chip], len(STAGES))

    held, out = None, None
    for s, names in enumerate(STAGES):
        for n in names:
            place = jnp.asarray([held_at[c][n] if held_at[c][n] >= 0 else stripes for c in range(chips)], jnp.int32)
            meta = jnp.stack([place[chip], core])
            other = lax.ppermute(b[n], "example", CORES)
            after = [] if out is None else [out]
            held = prepare(meta, b[n], other, inverse, inverse_other, held, after, stripes, height)
        out = grams(cov_scale, s, table, spans[s], *held, noise_tiles, out)
    return out


def plain_body(features, tile_lists, noise_tiles):
    slots, height, stripe = noise_tiles.shape
    rows = features.shape[0]
    chips = lax.axis_size("tile")
    stripes = features.shape[1] * chips // stripe
    core = lax.axis_index("example")
    cov_scale = F / math.sqrt(rows * lax.axis_size("example"))
    values = features.astype(jnp.float32)
    norms = lax.psum(jnp.sum(values * values, axis=1), "tile")
    inverse = (1.0 / jnp.maximum(jnp.sqrt(norms), math.sqrt(2.0 * F)))[:, None]
    scaled = (values * inverse).astype(jnp.bfloat16)
    wide = lax.all_gather(lax.all_gather(scaled, "tile", axis=1, tiled=True), "example", axis=0, tiled=True)
    right = wide.reshape(2 * rows, stripes, stripe).transpose(1, 0, 2)
    left = lax.dynamic_slice_in_dim(right, core * height, height, 2).transpose(0, 2, 1)
    first, second, living = slot_table(tile_lists, lax.axis_index("tile"), slots)
    table, spans = schedule(first, second, living, jnp.zeros((stripes,), jnp.int32), 1)
    return grams(cov_scale, 0, table, spans[0], right, left, noise_tiles, None)


def body(features, tile_lists, noise_tiles):
    if lax.axis_size("tile") == 8 and features.shape[1] == 2 * noise_tiles.shape[2]:
        return grid_body(features, tile_lists, noise_tiles)
    return plain_body(features, tile_lists, noise_tiles)


def solution(mesh):
    placed = (
        P(("groups", "example"), "tile"),
        P("groups", None),
        P(("groups", "tile"), "example", None),
    )
    return jax.shard_map(
        body,
        mesh=mesh,
        in_specs=placed,
        out_specs=P(("groups", "tile"), "example", None),
        check_vma=False,
    )
```

```python
import functools
import math

import jax
import jax.numpy as jnp
import numpy as np
from jax import lax
from jax.experimental import pallas as pl
from jax.experimental.pallas import tpu as pltpu
from jax.sharding import PartitionSpec as P

F = 8192
VMEM = 63 * 1024 * 1024
CORES = [(0, 1), (1, 0)]

SLOTS = 7


def partner(chip, along):
    z, y = chip // 2, chip % 2
    if along == "y":
        return 2 * z + 1 - y
    return 2 * ((z ^ 1) if along == "z" else 3 - z) + y


def is_end(chip):
    return chip // 2 in (0, 3)


def z_core(k):
    return ((k + 1) // 2) % 2


def slot_pairs(k):
    pairs = []
    for chip in range(8):
        c = z_core(k)
        pairs.append((2 * chip + c, 2 * partner(chip, "z") + c))
        if is_end(chip):
            pairs.append((2 * chip + 1 - c, 2 * partner(chip, "y") + 1 - c))
        elif k < SLOTS - 1:
            pairs.append((2 * chip + 1 - c, 2 * partner(chip, "m") + 1 - c))
    return pairs


Y_SWAP = [(chip, partner(chip, "y")) for chip in range(8)]
Y_EXTRA = [(2 * a + 1 - z_core(1), 2 * b + 1 - z_core(1)) for a, b in Y_SWAP if not is_end(a)]


def slot_table(tile_lists, owner, slots):
    owners = tile_lists[:, 2]
    entries = tile_lists.shape[0]
    position = jnp.arange(entries, dtype=jnp.int32)
    mine = owners == owner
    earlier = (position[None, :] < position[:, None]) & mine[None, :]
    ranks = jnp.sum(earlier.astype(jnp.int32), axis=1)
    matches = (
        mine[None, :] & (ranks[None, :] == jnp.arange(slots, dtype=jnp.int32)[:, None])
    ).astype(jnp.int32)
    living = jnp.sum(matches, axis=1)
    first = jnp.sum(matches * tile_lists[None, :, 0], axis=1)
    second = jnp.sum(matches * tile_lists[None, :, 1], axis=1)
    return (first, second, living)


MOST = 5


def numbers(stripes):
    inside = {}
    for chip in range(8):
        for core in range(2):
            inside[2 * chip + core] = 2 * chip + core
    got = {d: [] for d in inside}
    for k in range(SLOTS):
        sent = {d: (inside[d] if k < 2 else got[d][k - 2]) for d in inside}
        came = {b: sent[a] for a, b in slot_pairs(k)}
        for d in inside:
            got[d].append(came.get(d, stripes))
    table = np.full((16, 4 + 2 * SLOTS + stripes), stripes, np.int32)
    for d in inside:
        row = table[d]
        places = row[4 + 2 * SLOTS :]
        row[0:2] = inside[d], inside[d ^ 1]
        places[row[0]], places[row[1]] = 0, 1
        for k in range(SLOTS):
            for spot, stripe in enumerate((got[d][k], got[d ^ 1][k])):
                row[2 + 2 * k + spot] = stripe
                if stripe < stripes:
                    places[stripe] = 2 * k + spot
        chip = d // 2
        if not is_end(chip):
            stripe = got[2 * partner(chip, "y") + 1 - z_core(1)][1]
            spot = (d + 1 - z_core(1)) % 2
            row[2 + 2 * SLOTS + spot] = stripe
            places[stripe] = 2 * EXTRA + spot
        assert sorted(x for x in row[: 4 + 2 * SLOTS] if x < stripes) == list(range(stripes))
    return table


EXTRA = 5


def call(kernel, name, operands, scalars, results, scratch, aliases, after=()):
    hbm = pl.BlockSpec(memory_space=pltpu.HBM)
    operands = [*operands, *after]
    return pl.pallas_call(
        kernel,
        in_specs=[pl.BlockSpec(memory_space=pltpu.SMEM)] * scalars + [hbm] * (len(operands) - scalars),
        out_specs=[hbm] * len(results),
        out_shape=[jax.ShapeDtypeStruct(shape, dtype) for shape, dtype in results],
        scratch_shapes=scratch,
        input_output_aliases=aliases,
        compiler_params=pltpu.CompilerParams(vmem_limit_bytes=VMEM),
        cost_estimate=pl.CostEstimate(flops=1024, bytes_accessed=1024, transcendentals=0),
        name=name,
    )(*operands)


def keep(arrays, after):
    return call(
        lambda *_: None,
        "keep",
        arrays,
        0,
        [(x.shape, x.dtype) for x in arrays],
        [],
        {k: k for k in range(len(arrays))},
        after,
    )


def own_kernel(place, mine, other, whole, room, arrive, leave):
    core = place[0]
    rows, stripe = other.shape
    column = pl.ds(pl.multiple_of(core * stripe, stripe), stripe)
    source = [mine.at[:, column], other]
    side = [core, 1 - core]
    into = [pltpu.make_async_copy(source[k], room.at[k], arrive.at[k]) for k in range(2)]
    outof = [
        pltpu.make_async_copy(room.at[k], whole.at[pl.ds(side[k] * rows, rows)], leave.at[k]) for k in range(2)
    ]
    for copy in into:
        copy.start()
    for k in range(2):
        into[k].wait()
        outof[k].start()
    for copy in outof:
        copy.wait()


def own_stripe(place, mine, other):
    rows, stripe = other.shape
    return call(
        own_kernel,
        "own",
        [place, mine, other],
        1,
        [((2 * rows, stripe), jnp.bfloat16)],
        [
            pltpu.VMEM((2, rows, stripe), jnp.bfloat16),
            pltpu.SemaphoreType.DMA((2,)),
            pltpu.SemaphoreType.DMA((2,)),
        ],
        {},
    )[0]


def unpack_kernel(spots, stripes, meta, inverse, *rest):
    n = len(spots)
    raws = rest[:n]
    held, halves = rest[-7 - 2 * n], rest[-6 - 2 * n : -6]
    taken, given, scales, arrive, leave, wide = rest[-6:]
    depth = held.shape[1]
    rows = depth // 2
    part = rows // 2
    side = [pl.ds(h * rows, rows) for h in range(2)]
    into = lambda k, h: pltpu.make_async_copy(raws[k].at[side[h]], taken.at[k, side[h]], arrive.at[2 * k + h])

    def outof(k, h):
        piece = given.at[k, side[h]]
        place = held.at[meta[spots[k]], side[h]]
        return (
            pltpu.make_async_copy(piece, halves[2 * k + h], leave.at[2 * (2 * k + h)]),
            pltpu.make_async_copy(piece, place, leave.at[2 * (2 * k + h) + 1]),
        )

    def each(step):
        for k in range(n):

            @pl.when(meta[spots[k]] < stripes)
            def _(k=k):
                for h in range(2):
                    step(k, h)

    def scale(k, h):
        into(k, h).wait()

        @pl.loop(0, 2)
        def _(r):
            at = pl.ds(pl.multiple_of(h * rows + r * part, part), part)
            given[k, at] = (taken[k, at].astype(jnp.float32) * scales[at, :1]).astype(jnp.bfloat16)

        for copy in outof(k, h):
            copy.start()

    def finish(k, h):
        for copy in outof(k, h):
            copy.wait()

    factors = pltpu.make_async_copy(inverse, scales, wide)
    factors.start()
    each(lambda k, h: into(k, h).start())
    factors.wait()
    each(scale)
    each(finish)


def unpack(spots, raws, meta, inverse, shape, held):
    n = len(spots)
    stripes, depth, stripe = shape
    half = ((depth // 2, stripe), jnp.bfloat16)
    given, aliases = [meta, inverse, *raws], {}
    if held is not None:
        aliases[len(given)] = 0
        given.append(held)
    held, *halves = call(
        functools.partial(unpack_kernel, spots, stripes),
        "unpack",
        given,
        1,
        [(shape, jnp.bfloat16)] + [half] * (2 * n),
        [
            pltpu.VMEM((n, depth, stripe), jnp.bfloat16),
            pltpu.VMEM((n, depth, stripe), jnp.bfloat16),
            pltpu.VMEM(inverse.shape, jnp.float32),
            pltpu.SemaphoreType.DMA((2 * n,)),
            pltpu.SemaphoreType.DMA((4 * n,)),
            pltpu.SemaphoreType.DMA(()),
        ],
        aliases,
    )
    return held, halves


def stage_kernel(cov_scale, stage, spots, stripes, meta, lefts, rights, slots, spans, noise, *rest):
    halves = rest[: 2 * len(spots)]
    held, out, room, zeros, arrive, leave, fill = rest[-7:]
    _, height, stripe = out.shape
    depth = held.shape[1]
    dead, here, begin, end = spans[0], spans[1], spans[2 + 2 * stage], spans[3 + 2 * stage]

    def each(step):
        for k, x in enumerate(halves):
            place = meta[spots[k // 2]]
            side = pl.ds((k % 2) * (depth // 2), depth // 2)
            into = pltpu.make_async_copy(x, room.at[k], arrive.at[k])
            outof = pltpu.make_async_copy(room.at[k], held.at[place, side], leave.at[k])
            pl.when(place < stripes)(functools.partial(step, into, outof))

    def pass_on(into, outof):
        into.wait()
        outof.start()

    each(lambda into, outof: into.start())
    each(pass_on)
    each(lambda into, outof: outof.wait())

    def clear(e):
        return pltpu.make_async_copy(zeros, out.at[slots[e]], fill)

    if stage == 0:

        @pl.when(dead > 0)
        def _():
            zeros[...] = jnp.zeros_like(zeros)
            pl.loop(0, dead)(lambda e: clear(e).start())
            pl.loop(0, dead)(lambda e: clear(e).wait())

    def one_tile(l, r, n, o):
        gram = lax.dot_general(l[0], r[0], (((0,), (0,)), ((), ())), preferred_element_type=jnp.float32)
        o[0] = cov_scale * gram + n[0]

    @pl.when(end > begin)
    def _():
        pltpu.emit_pipeline(
            one_tile,
            grid=(end - begin,),
            in_specs=[
                pl.BlockSpec((1, depth, height), lambda e: (lefts[begin + e], 0, here)),
                pl.BlockSpec((1, depth, stripe), lambda e: (rights[begin + e], 0, 0)),
                pl.BlockSpec((1, height, stripe), lambda e: (slots[begin + e], 0, 0)),
            ],
            out_specs=[pl.BlockSpec((1, height, stripe), lambda e: (slots[begin + e], 0, 0))],
        )(held, held, noise, out)


def run_stage(cov_scale, stage, spots, halves, meta, table, spans, noise, held, out):
    slots, height, stripe = noise.shape
    stripes, depth = held.shape[:2]
    moves = max(len(halves), 1)
    given = [meta, *table, spans, noise, *halves, held]
    aliases = {len(given) - 1: 0}
    if out is not None:
        aliases[len(given)] = 1
        given.append(out)
    return call(
        functools.partial(stage_kernel, cov_scale, stage, spots, stripes),
        "stage",
        given,
        5,
        [(held.shape, jnp.bfloat16), (noise.shape, jnp.float32)],
        [
            pltpu.VMEM((moves, depth // 2, stripe), jnp.bfloat16),
            pltpu.VMEM((height, stripe), jnp.float32),
            pltpu.SemaphoreType.DMA((moves,)),
            pltpu.SemaphoreType.DMA((moves,)),
            pltpu.SemaphoreType.DMA(()),
        ],
        aliases,
    )


def schedule(first, second, living, stage_of, stages, core):
    slots = first.shape[0]
    look = lambda index: jnp.sum(
        jnp.where(index[:, None] == jnp.arange(stage_of.shape[0])[None, :], stage_of[None, :], 0), axis=1
    )
    stage = jnp.where(living > 0, jnp.maximum(look(first), look(second)), -1)
    position = jnp.arange(slots, dtype=jnp.int32)
    key = (((stage + 1) * 64 + second) * 64 + first) * slots + position
    rank = jnp.sum((key[None, :] < key[:, None]).astype(jnp.int32), axis=1)
    pick = (rank[None, :] == position[:, None]).astype(jnp.int32)
    put = lambda values: jnp.sum(pick * values[None, :], axis=1)
    table = (put(first), put(second), put(position))
    dead = jnp.sum((living == 0).astype(jnp.int32))
    ready = jnp.sum((stage[None, :] <= jnp.arange(stages)[:, None]).astype(jnp.int32), axis=1)
    spans, begin = [dead, core], dead
    for step in range(stages):
        end = ready[step] if step >= stages - 2 else jnp.minimum(ready[step], begin + MOST)
        spans += [begin, end]
        begin = end
    return table, jnp.stack(spans).astype(jnp.int32)


def grid_body(features, tile_lists, noise_tiles):
    slots, height, stripe = noise_tiles.shape
    rows = features.shape[0]
    chips = lax.axis_size("tile")
    stripes = features.shape[1] * chips // stripe
    shape = (stripes, 2 * rows, stripe)
    chip = lax.axis_index("tile")
    core = lax.axis_index("example").astype(jnp.int32)
    cov_scale = F / math.sqrt(rows * lax.axis_size("example"))
    slot = lambda k, x: lax.ppermute(x, ("tile", "example"), slot_pairs(k))
    swap = lambda x: lax.ppermute(x, "example", CORES)

    joint = lambda x, pairs: lax.ppermute(x, ("tile", "example"), pairs)
    place = core.reshape(1)

    rows_other = swap(jnp.where(core == 0, features[:, stripe:], features[:, :stripe]))
    raw = own_stripe(place, features, rows_other)
    first_sent = slot(0, raw)

    values = features.astype(jnp.float32)
    squares = jnp.sum(values * values, axis=1)
    squares_other = swap(squares)
    both = jnp.where(core == 0, jnp.stack([squares, squares_other]), jnp.stack([squares_other, squares]))
    [both] = keep([both], [raw])
    both = both + joint(both, [(2 * a, 2 * b) for a, b in Y_SWAP])
    both = jnp.where(core == 0, both, swap(both))
    norms = both
    for k in (1, 2, 3):
        source = lambda c: 2 * c + (0 if k > 1 and not is_end(c) else 1)
        norms = norms + joint(both, [(source(c), 2 * (c ^ (2 * k)) + 1) for c in range(chips)])
    [later] = keep([raw], [norms])
    norms = jnp.where(core == 1, norms, swap(norms)).reshape(2 * rows)
    inverse = 1.0 / jnp.maximum(jnp.sqrt(norms), math.sqrt(2.0 * F))
    inverse = jnp.broadcast_to(inverse[:, None], (2 * rows, 128))

    meta = lax.dynamic_index_in_dim(jnp.asarray(numbers(stripes)), 2 * chip + core, 0, keepdims=False)
    first, second, living = slot_table(tile_lists, chip, slots)
    table, spans = schedule(first, second, living, meta[4 + 2 * SLOTS :], 2 * SLOTS, core)

    come = [first_sent, slot(1, later)]
    held = out = extra = None
    for k in range(SLOTS):
        spots, raws = [2 + 2 * k], [come[k]]
        if k == 0:
            spots, raws = [0] + spots, [later] + raws
            come.append(slot(2, come[0]))
        elif k % 2 == 0 and k + 2 < SLOTS:
            come[k - 1], come[k] = keep([come[k - 1], come[k]], [out])
            come += [slot(k + 1, come[k - 1]), slot(k + 2, come[k])]
            raws = [come[k]]
            if k == 2:
                extra = joint(come[1], Y_EXTRA)
        if k == EXTRA:
            spots, raws = spots + [2 + 2 * SLOTS], raws + [extra]
        held, halves = unpack(spots, raws, meta, inverse, shape, held)
        halves = [swap(x) for x in halves]
        tiles = functools.partial(run_stage, meta=meta, table=table, spans=spans, noise=noise_tiles)
        held, out = tiles(cov_scale, 2 * k, [], [], held=held, out=out)
        held, out = tiles(cov_scale, 2 * k + 1, [s + 1 for s in spots], halves, held=held, out=out)
    return out


def plain_body(features, tile_lists, noise_tiles):
    slots, height, stripe = noise_tiles.shape
    rows = features.shape[0]
    chips = lax.axis_size("tile")
    stripes = features.shape[1] * chips // stripe
    core = lax.axis_index("example").astype(jnp.int32)
    cov_scale = F / math.sqrt(rows * lax.axis_size("example"))
    values = features.astype(jnp.float32)
    norms = lax.psum(jnp.sum(values * values, axis=1), "tile")
    inverse = (1.0 / jnp.maximum(jnp.sqrt(norms), math.sqrt(2.0 * F)))[:, None]
    scaled = (values * inverse).astype(jnp.bfloat16)
    wide = lax.all_gather(lax.all_gather(scaled, "tile", axis=1, tiled=True), "example", axis=0, tiled=True)
    held = wide.reshape(2 * rows, stripes, stripe).transpose(1, 0, 2)
    first, second, living = slot_table(tile_lists, lax.axis_index("tile"), slots)
    table, spans = schedule(first, second, living, jnp.zeros((stripes,), jnp.int32), 1, core)
    meta = jnp.zeros((1,), jnp.int32)
    return run_stage(cov_scale, 0, [], [], meta, table, spans, noise_tiles, held, None)[1]


def body(features, tile_lists, noise_tiles):
    if lax.axis_size("tile") == 8 and features.shape[1] == 2 * noise_tiles.shape[2]:
        return grid_body(features, tile_lists, noise_tiles)
    return plain_body(features, tile_lists, noise_tiles)


def solution(mesh):
    placed = (
        P(("groups", "example"), "tile"),
        P("groups", None),
        P(("groups", "tile"), "example", None),
    )
    return jax.shard_map(
        body,
        mesh=mesh,
        in_specs=placed,
        out_specs=P(("groups", "tile"), "example", None),
        check_vma=False,
    )
```

```python
import functools
import math

import jax
import jax.numpy as jnp
import numpy as np
from jax import lax
from jax.experimental import pallas as pl
from jax.experimental.pallas import tpu as pltpu
from jax.sharding import PartitionSpec as P

F = 8192
VMEM = 63 * 1024 * 1024
CORES = [(0, 1), (1, 0)]

SLOTS = 7


def partner(chip, along):
    z, y = chip // 2, chip % 2
    if along == "y":
        return 2 * z + 1 - y
    return 2 * ((z ^ 1) if along == "z" else 3 - z) + y


def is_end(chip):
    return chip // 2 in (0, 3)


def z_core(k):
    return ((k + 1) // 2) % 2


def slot_pairs(k):
    c = z_core(k)
    pairs = []
    for chip in range(8):
        pairs.append((2 * chip + c, 2 * partner(chip, "z") + c))
        pairs.append((2 * chip + 1 - c, 2 * partner(chip, "y" if is_end(chip) else "m") + 1 - c))
    return pairs


Y_SWAP = [(chip, partner(chip, "y")) for chip in range(8)]


def slot_table(tile_lists, owner, slots):
    owners = tile_lists[:, 2]
    entries = tile_lists.shape[0]
    position = jnp.arange(entries, dtype=jnp.int32)
    mine = owners == owner
    earlier = (position[None, :] < position[:, None]) & mine[None, :]
    ranks = jnp.sum(earlier.astype(jnp.int32), axis=1)
    matches = (
        mine[None, :] & (ranks[None, :] == jnp.arange(slots, dtype=jnp.int32)[:, None])
    ).astype(jnp.int32)
    living = jnp.sum(matches, axis=1)
    first = jnp.sum(matches * tile_lists[None, :, 0], axis=1)
    second = jnp.sum(matches * tile_lists[None, :, 1], axis=1)
    return (first, second, living)


AHEAD, BEHIND, CLEAR = 6, 4, 4

EVENTS = ["own", 0, 1, 2, 3, 4, 5, 6]


def numbers(stripes):
    devices = range(16)
    got = {d: [] for d in devices}
    for k in range(SLOTS):
        sent = {d: (d if k < 2 else got[d][k - 2]) for d in devices}
        for a, b in slot_pairs(k):
            got[b].append(sent[a])
    table = np.zeros((16, 2 * len(EVENTS) + stripes), np.int32)
    for d in devices:
        row = table[d]
        places = row[2 * len(EVENTS) :]
        for k, event in enumerate(EVENTS):
            for j, who in enumerate((d, d ^ 1)):
                if event == "own":
                    stripe = who
                else:
                    stripe = got[who][event]
                row[2 * k + j] = stripe
                places[stripe] = 2 * k + j
        assert sorted(row[: 2 * len(EVENTS)]) == list(range(stripes))
    return table


def call(kernel, name, operands, scalars, results, scratch, aliases, after=(), space=pltpu.HBM):
    hbm = pl.BlockSpec(memory_space=space)
    operands = [*operands, *after]
    return pl.pallas_call(
        kernel,
        in_specs=[pl.BlockSpec(memory_space=pltpu.SMEM)] * scalars + [hbm] * (len(operands) - scalars),
        out_specs=[hbm] * len(results),
        out_shape=[jax.ShapeDtypeStruct(shape, dtype) for shape, dtype in results],
        scratch_shapes=scratch,
        input_output_aliases=aliases,
        compiler_params=pltpu.CompilerParams(vmem_limit_bytes=VMEM),
        cost_estimate=pl.CostEstimate(flops=1024, bytes_accessed=1024, transcendentals=0),
        name=name,
    )(*operands)


def keep(arrays, after):
    return call(
        lambda *_: None,
        "keep",
        arrays,
        0,
        [(x.shape, x.dtype) for x in arrays],
        [],
        {k: k for k in range(len(arrays))},
        after,
    )


def own_kernel(place, mine, other, *rest):
    whole, room, arrive, leave = rest[-4:]
    core = place[0]
    rows, stripe = other.shape
    pieces = arrive.shape[0] // 2
    part = rows // pieces
    column = pl.ds(pl.multiple_of(core * stripe, stripe), stripe)
    copies = []
    for k, side in enumerate((core, 1 - core)):
        for r in range(pieces):
            at = pl.ds(r * part, part)
            target = pl.ds(pl.multiple_of(side * rows + r * part, part), part)
            source = mine.at[at, column] if k == 0 else other.at[at]
            spot = pieces * k + r
            copies.append((
                pltpu.make_async_copy(source, room.at[k, at], arrive.at[spot]),
                pltpu.make_async_copy(room.at[k, at], whole.at[target], leave.at[spot]),
            ))
    for into, _ in copies:
        into.start()
    for into, outof in copies:
        into.wait()
        outof.start()
    for _, outof in copies:
        outof.wait()


def own_stripe(place, mine, other, after):
    rows, stripe = other.shape
    return call(
        own_kernel,
        "own",
        [place, mine, other],
        1,
        [((2 * rows, stripe), jnp.bfloat16)],
        [
            pltpu.VMEM((2, rows, stripe), jnp.bfloat16),
            pltpu.SemaphoreType.DMA((4,)),
            pltpu.SemaphoreType.DMA((4,)),
        ],
        {},
        after,
        pl.ANY,
    )[0]


def unpack_kernel(event, meta, inverse, raw, *rest):
    held, *halves = rest[-9:-6]
    taken, given, scales, arrive, leave, wide = rest[-6:]
    depth = held.shape[1]
    pieces = arrive.shape[0]
    part = depth // pieces
    place = meta[2 * event]

    def rows(r):
        return pl.ds(r * part, part)

    def into(r):
        return [
            pltpu.make_async_copy(raw.at[rows(r)], taken.at[rows(r)], arrive.at[r]),
            pltpu.make_async_copy(inverse.at[rows(r)], scales.at[rows(r)], wide.at[r]),
        ]

    def outof(r):
        half = pieces // 2
        return [
            pltpu.make_async_copy(given.at[rows(r)], halves[r // half].at[rows(r % half)], leave.at[2 * r]),
            pltpu.make_async_copy(given.at[rows(r)], held.at[place, rows(r)], leave.at[2 * r + 1]),
        ]

    for r in range(pieces):
        for copy in into(r):
            copy.start()
    for r in range(pieces):
        for copy in into(r):
            copy.wait()
        given[rows(r)] = (taken[rows(r)].astype(jnp.float32) * scales[rows(r), :1]).astype(jnp.bfloat16)
        for copy in outof(r):
            copy.start()
    for r in range(pieces):
        for copy in outof(r):
            copy.wait()


def unpack(event, raw, meta, inverse, shape, held):
    stripes, depth, stripe = shape
    half = ((depth // 2, stripe), jnp.bfloat16)
    pieces = 8
    given, aliases = [meta, inverse, raw], {}
    if held is not None:
        aliases[len(given)] = 0
        given.append(held)
    held, *halves = call(
        functools.partial(unpack_kernel, event),
        "unpack",
        given,
        1,
        [(shape, jnp.bfloat16), half, half],
        [
            pltpu.VMEM((depth, stripe), jnp.bfloat16),
            pltpu.VMEM((depth, stripe), jnp.bfloat16),
            pltpu.VMEM(inverse.shape, jnp.float32),
            pltpu.SemaphoreType.DMA((pieces,)),
            pltpu.SemaphoreType.DMA((2 * pieces,)),
            pltpu.SemaphoreType.DMA((pieces,)),
        ],
        aliases,
    )
    return held, halves


def dot(left, right):
    return lax.dot_general(left, right, (((0,), (0,)), ((), ())), preferred_element_type=jnp.float32)


def stage_kernel(cov_scale, stage, given, last, meta, lefts, rights, slots, spans, noise, *rest):
    given = rest[:given]
    held, out, lbuf, rbuf, noises, outs, zeros, arrive, leave, streamed, noised, stored, fill = rest[-13:]
    _, height, stripe = out.shape
    depth = held.shape[1]
    rows = depth // 2
    ahead, behind = noises.shape[0], outs.shape[0]
    dead, here, begin, middle, end = spans[0], spans[1], *(spans[2 + 2 * stage + k] for k in range(3))
    place = meta[stage]
    columns = pl.ds(pl.multiple_of(here * height, height), height)
    sides = [pl.ds(h * rows, rows) for h in range(2)]
    sources = given or [held.at[place, side] for side in sides]
    into = [pltpu.make_async_copy(sources[h], rbuf.at[0, sides[h]], arrive.at[h]) for h in range(2)]
    outof = [pltpu.make_async_copy(rbuf.at[0, side], held.at[place, side], leave.at[h]) for h, side in enumerate(sides)]

    def clear(e):
        return pltpu.make_async_copy(zeros, out.at[slots[e]], fill)

    def by_row(e):
        return e < middle

    def by_column(e):
        return (e >= middle) & (lefts[e] != rights[e])

    def fetch(e, step):
        b = lax.rem(e - begin, ahead)
        step(pltpu.make_async_copy(noise.at[slots[e]], noises.at[b], noised.at[b]))
        right = pltpu.make_async_copy(held.at[rights[e]], rbuf.at[1 + b], streamed.at[b])
        left = pltpu.make_async_copy(held.at[lefts[e], :, columns], lbuf.at[1 + b], streamed.at[b])
        pl.when(by_row(e))(lambda: step(right))
        pl.when(by_column(e))(lambda: step(left))

    def store(e):
        o = lax.rem(e - begin, behind)
        return pltpu.make_async_copy(outs.at[o], out.at[slots[e]], stored.at[o])

    def one_tile(e):
        b, o = lax.rem(e - begin, ahead), lax.rem(e - begin, behind)
        fetch(e, lambda copy: copy.wait())
        pl.when(e - begin >= behind)(lambda: store(e).wait())
        left = lbuf[jnp.where(by_column(e), 1 + b, 0)]
        right = rbuf[jnp.where(by_row(e), 1 + b, 0)]
        outs[o] = cov_scale * dot(left, right) + noises[b]
        store(e).start()
        pl.when(e + ahead < end)(lambda: fetch(e + ahead, lambda copy: copy.start()))

    if stage == CLEAR:

        @pl.when(dead > 0)
        def _():
            zeros[...] = jnp.zeros_like(zeros)
            pl.loop(0, dead)(lambda e: clear(e).start())

    @pl.when((end > begin) | (len(given) > 0 and not last))
    def _():
        for copy in into:
            copy.start()
        pl.loop(begin, jnp.minimum(begin + ahead, end))(lambda e: fetch(e, lambda copy: copy.start()))
        for copy in into:
            copy.wait()
        if given and not last:
            for copy in outof:
                copy.start()

        @pl.when(end > begin)
        def _():
            lbuf[0] = rbuf[0, :, columns]
            pl.loop(begin, end)(one_tile)
            pl.loop(jnp.maximum(end - behind, begin), end)(lambda e: store(e).wait())

        if given and not last:
            for copy in outof:
                copy.wait()

    if stage == CLEAR:
        pl.when(dead > 0)(lambda: pl.loop(0, dead)(lambda e: clear(e).wait()))


def run_stage(cov_scale, stage, halves, meta, table, spans, noise, held, out):
    slots, height, stripe = noise.shape
    stripes, depth = held.shape[:2]
    given = [meta, *table, spans, noise, *halves, held]
    aliases = {len(given) - 1: 0}
    if out is not None:
        aliases[len(given)] = 1
        given.append(out)
    return call(
        functools.partial(stage_kernel, cov_scale, stage, len(halves), stage == 2 * len(EVENTS) - 1),
        "stage",
        given,
        5,
        [(held.shape, jnp.bfloat16), (noise.shape, jnp.float32)],
        [
            pltpu.VMEM((1 + AHEAD, depth, height), jnp.bfloat16),
            pltpu.VMEM((1 + AHEAD, depth, stripe), jnp.bfloat16),
            pltpu.VMEM((AHEAD, height, stripe), jnp.float32),
            pltpu.VMEM((BEHIND, height, stripe), jnp.float32),
            pltpu.VMEM((height, stripe), jnp.float32),
            pltpu.SemaphoreType.DMA((2,)),
            pltpu.SemaphoreType.DMA((2,)),
            pltpu.SemaphoreType.DMA((AHEAD,)),
            pltpu.SemaphoreType.DMA((AHEAD,)),
            pltpu.SemaphoreType.DMA((BEHIND,)),
            pltpu.SemaphoreType.DMA(()),
        ],
        aliases,
    )


def plain_kernel(cov_scale, lefts, rights, slots, spans, noise, held, out, zeros, fill):
    _, height, stripe = out.shape
    depth = held.shape[1]
    dead, here, end = spans[0], spans[1], spans[4]

    def clear(e):
        return pltpu.make_async_copy(zeros, out.at[slots[e]], fill)

    def one_tile(l, r, n, o):
        o[0] = cov_scale * dot(l[0], r[0]) + n[0]

    @pl.when(dead > 0)
    def _():
        zeros[...] = jnp.zeros_like(zeros)
        pl.loop(0, dead)(lambda e: clear(e).start())
        pl.loop(0, dead)(lambda e: clear(e).wait())

    tile = pl.BlockSpec((1, height, stripe), lambda e: (slots[dead + e], 0, 0))
    left = pl.BlockSpec((1, depth, height), lambda e: (lefts[dead + e], 0, here))
    right = pl.BlockSpec((1, depth, stripe), lambda e: (rights[dead + e], 0, 0))
    pl.when(end > dead)(
        lambda: pltpu.emit_pipeline(
            one_tile, grid=(end - dead,), in_specs=[left, right, tile], out_specs=[tile]
        )(held, held, noise, out)
    )


def schedule(first, second, living, stage_of, stages, core):
    slots = first.shape[0]
    look = lambda index: jnp.sum(
        jnp.where(index[:, None] == jnp.arange(stage_of.shape[0])[None, :], stage_of[None, :], 0), axis=1
    )
    one, two = look(first), look(second)
    stage = jnp.where(living > 0, 2 * jnp.maximum(one, two) + (two >= one).astype(jnp.int32), -1)
    position = jnp.arange(slots, dtype=jnp.int32)
    key = ((stage + 1) * 64 + second) * slots + position
    rank = jnp.sum((key[None, :] < key[:, None]).astype(jnp.int32), axis=1)
    pick = (rank[None, :] == position[:, None]).astype(jnp.int32)
    put = lambda values: jnp.sum(pick * values[None, :], axis=1)
    table = (put(first), put(second), put(position))
    bounds = jnp.sum((stage[None, :] < jnp.arange(2 * stages + 1)[:, None]).astype(jnp.int32), axis=1)
    return table, jnp.concatenate([bounds[:1], core.reshape(1), bounds]).astype(jnp.int32)


def grid_body(features, tile_lists, noise_tiles):
    slots, height, stripe = noise_tiles.shape
    rows = features.shape[0]
    chips = lax.axis_size("tile")
    stripes = features.shape[1] * chips // stripe
    shape = (stripes, 2 * rows, stripe)
    chip = lax.axis_index("tile")
    core = lax.axis_index("example").astype(jnp.int32)
    cov_scale = F / math.sqrt(rows * lax.axis_size("example"))
    slot = lambda k, x: lax.ppermute(x, ("tile", "example"), slot_pairs(k))
    swap = lambda x: lax.ppermute(x, "example", CORES)

    joint = lambda x, pairs: lax.ppermute(x, ("tile", "example"), pairs)
    place = core.reshape(1)

    rows_other = swap(lax.dynamic_slice_in_dim(features, (1 - core) * stripe, stripe, 1))
    values = features.astype(jnp.float32)
    squares = jnp.sum(values * values, axis=1)
    squares_y = lax.ppermute(squares, "tile", Y_SWAP)
    raw = own_stripe(place, features, rows_other, [squares_y])
    first_sent = slot(0, raw)
    squares = squares + squares_y
    squares_other = swap(squares)
    both = jnp.where(core == 0, jnp.stack([squares, squares_other]), jnp.stack([squares_other, squares]))
    norms = both
    for k in (1, 2, 3):
        source = lambda c: 2 * c + (0 if k > 1 and not is_end(c) else 1)
        norms = norms + joint(both, [(source(c), 2 * (c ^ (2 * k)) + 1) for c in range(chips)])
    [later] = keep([raw], [norms])
    norms = jnp.where(core == 1, norms, swap(norms)).reshape(2 * rows)
    inverse = 1.0 / jnp.maximum(jnp.sqrt(norms), math.sqrt(2.0 * F))
    inverse = jnp.broadcast_to(inverse[:, None], (2 * rows, 128))

    meta = lax.dynamic_index_in_dim(jnp.asarray(numbers(stripes)), 2 * chip + core, 0, keepdims=False)
    first, second, living = slot_table(tile_lists, chip, slots)
    table, spans = schedule(first, second, living, meta[2 * len(EVENTS) :], 2 * len(EVENTS), core)

    come = [first_sent, slot(1, later)]
    held = out = None
    for k, event in enumerate(EVENTS):
        raw = later if event == "own" else come[event]
        if event in (0, 2, 4):
            come.append(slot(event + 2, raw))
        held, halves = unpack(k, raw, meta, inverse, shape, held)
        halves = [swap(x) for x in halves]
        held, out = run_stage(cov_scale, 2 * k, [], meta, table, spans, noise_tiles, held, out)
        held, out = run_stage(cov_scale, 2 * k + 1, halves, meta, table, spans, noise_tiles, held, out)
        if event == "own":
            [come[0]] = keep([come[0]], [out])
        if event in (1, 3):
            [come[event]] = keep([come[event]], [out])
            come.append(slot(event + 2, come[event]))
    return out


def plain_body(features, tile_lists, noise_tiles):
    slots, height, stripe = noise_tiles.shape
    rows = features.shape[0]
    chips = lax.axis_size("tile")
    stripes = features.shape[1] * chips // stripe
    core = lax.axis_index("example").astype(jnp.int32)
    cov_scale = F / math.sqrt(rows * lax.axis_size("example"))
    values = features.astype(jnp.float32)
    norms = lax.psum(jnp.sum(values * values, axis=1), "tile")
    inverse = (1.0 / jnp.maximum(jnp.sqrt(norms), math.sqrt(2.0 * F)))[:, None]
    scaled = (values * inverse).astype(jnp.bfloat16)
    wide = lax.all_gather(lax.all_gather(scaled, "tile", axis=1, tiled=True), "example", axis=0, tiled=True)
    held = wide.reshape(2 * rows, stripes, stripe).transpose(1, 0, 2)
    first, second, living = slot_table(tile_lists, lax.axis_index("tile"), slots)
    table, spans = schedule(first, second, living, jnp.zeros((stripes,), jnp.int32), 1, core)
    return call(
        functools.partial(plain_kernel, cov_scale),
        "plain",
        [*table, spans, noise_tiles, held],
        4,
        [(noise_tiles.shape, jnp.float32)],
        [pltpu.VMEM((height, stripe), jnp.float32), pltpu.SemaphoreType.DMA(())],
        {},
    )[0]


def body(features, tile_lists, noise_tiles):
    if lax.axis_size("tile") == 8 and features.shape[1] == 2 * noise_tiles.shape[2]:
        return grid_body(features, tile_lists, noise_tiles)
    return plain_body(features, tile_lists, noise_tiles)


def solution(mesh):
    placed = (
        P(("groups", "example"), "tile"),
        P("groups", None),
        P(("groups", "tile"), "example", None),
    )
    return jax.shard_map(
        body,
        mesh=mesh,
        in_specs=placed,
        out_specs=P(("groups", "tile"), "example", None),
        check_vma=False,
    )
```

```python
import functools
import math

import jax
import jax.numpy as jnp
import numpy as np
from jax import lax
from jax.experimental import pallas as pl
from jax.experimental.pallas import tpu as pltpu
from jax.sharding import PartitionSpec as P

F = 8192
VMEM = 63 * 1024 * 1024
CORES = [(0, 1), (1, 0)]

SLOTS = 7


def partner(chip, along):
    z, y = chip // 2, chip % 2
    if along == "y":
        return 2 * z + 1 - y
    return 2 * ((z ^ 1) if along == "z" else 3 - z) + y


def is_end(chip):
    return chip // 2 in (0, 3)


def z_core(k):
    return ((k + 1) // 2) % 2


def slot_pairs(k):
    c = z_core(k)
    pairs = []
    for chip in range(8):
        pairs.append((2 * chip + c, 2 * partner(chip, "z") + c))
        pairs.append((2 * chip + 1 - c, 2 * partner(chip, "y" if is_end(chip) else "m") + 1 - c))
    return pairs


Y_SWAP = [(chip, partner(chip, "y")) for chip in range(8)]


def slot_table(tile_lists, owner, slots):
    owners = tile_lists[:, 2]
    entries = tile_lists.shape[0]
    position = jnp.arange(entries, dtype=jnp.int32)
    mine = owners == owner
    earlier = (position[None, :] < position[:, None]) & mine[None, :]
    ranks = jnp.sum(earlier.astype(jnp.int32), axis=1)
    matches = (
        mine[None, :] & (ranks[None, :] == jnp.arange(slots, dtype=jnp.int32)[:, None])
    ).astype(jnp.int32)
    living = jnp.sum(matches, axis=1)
    first = jnp.sum(matches * tile_lists[None, :, 0], axis=1)
    second = jnp.sum(matches * tile_lists[None, :, 1], axis=1)
    return (first, second, living)


AHEAD, BEHIND, CLEAR = 6, 4, 4

EVENTS = ["own", 0, 1, 2, 3, 4, 5, 6]


def numbers(stripes):
    devices = range(16)
    got = {d: [] for d in devices}
    for k in range(SLOTS):
        sent = {d: (d if k < 2 else got[d][k - 2]) for d in devices}
        for a, b in slot_pairs(k):
            got[b].append(sent[a])
    table = np.zeros((16, 2 * len(EVENTS) + stripes), np.int32)
    for d in devices:
        row = table[d]
        places = row[2 * len(EVENTS) :]
        for k, event in enumerate(EVENTS):
            for j, who in enumerate((d, d ^ 1)):
                if event == "own":
                    stripe = who
                else:
                    stripe = got[who][event]
                row[2 * k + j] = stripe
                places[stripe] = 2 * k + j
        assert sorted(row[: 2 * len(EVENTS)]) == list(range(stripes))
    return table


def call(kernel, name, operands, scalars, results, scratch, aliases, after=(), space=pltpu.HBM):
    hbm = pl.BlockSpec(memory_space=space)
    operands = [*operands, *after]
    return pl.pallas_call(
        kernel,
        in_specs=[pl.BlockSpec(memory_space=pltpu.SMEM)] * scalars + [hbm] * (len(operands) - scalars),
        out_specs=[hbm] * len(results),
        out_shape=[jax.ShapeDtypeStruct(shape, dtype) for shape, dtype in results],
        scratch_shapes=scratch,
        input_output_aliases=aliases,
        compiler_params=pltpu.CompilerParams(vmem_limit_bytes=VMEM),
        cost_estimate=pl.CostEstimate(flops=1024, bytes_accessed=1024, transcendentals=0),
        name=name,
    )(*operands)


def keep(arrays, after):
    return call(
        lambda *_: None,
        "keep",
        arrays,
        0,
        [(x.shape, x.dtype) for x in arrays],
        [],
        {k: k for k in range(len(arrays))},
        after,
    )


def merge_kernel(place, mine, other, *rest):
    whole, room, arrive, leave = rest[-4:]
    core = place[0]
    rows, stripe = other.shape
    pieces = arrive.shape[0] // 2
    part = rows // pieces
    copies = []
    for k, (source, side) in enumerate(((mine, core), (other, 1 - core))):
        for r in range(pieces):
            at = pl.ds(r * part, part)
            target = pl.ds(pl.multiple_of(side * rows + r * part, part), part)
            spot = pieces * k + r
            copies.append((
                pltpu.make_async_copy(source.at[at], room.at[k, at], arrive.at[spot]),
                pltpu.make_async_copy(room.at[k, at], whole.at[target], leave.at[spot]),
            ))
    for into, _ in copies:
        into.start()
    for into, outof in copies:
        into.wait()
        outof.start()
    for _, outof in copies:
        outof.wait()


def merge(place, mine, other, after=()):
    rows, stripe = other.shape
    return call(
        merge_kernel,
        "merge",
        [place, mine, other],
        1,
        [((2 * rows, stripe), jnp.bfloat16)],
        [
            pltpu.VMEM((2, rows, stripe), jnp.bfloat16),
            pltpu.SemaphoreType.DMA((4,)),
            pltpu.SemaphoreType.DMA((4,)),
        ],
        {},
        after,
    )[0]


def unpack_kernel(event, meta, inverse, raw, *rest):
    held, *halves = rest[-9:-6]
    taken, given, scales, arrive, leave, wide = rest[-6:]
    depth = held.shape[1]
    pieces = arrive.shape[0]
    part = depth // pieces
    place = meta[2 * event]

    def rows(r):
        return pl.ds(r * part, part)

    def into(r):
        return [
            pltpu.make_async_copy(raw.at[rows(r)], taken.at[rows(r)], arrive.at[r]),
            pltpu.make_async_copy(inverse.at[rows(r)], scales.at[rows(r)], wide.at[r]),
        ]

    def outof(r):
        half = pieces // 2
        return [
            pltpu.make_async_copy(given.at[rows(r)], halves[r // half].at[rows(r % half)], leave.at[2 * r]),
            pltpu.make_async_copy(given.at[rows(r)], held.at[place, rows(r)], leave.at[2 * r + 1]),
        ]

    for r in range(pieces):
        for copy in into(r):
            copy.start()
    for r in range(pieces):
        for copy in into(r):
            copy.wait()
        given[rows(r)] = (taken[rows(r)].astype(jnp.float32) * scales[rows(r), :1]).astype(jnp.bfloat16)
        for copy in outof(r):
            copy.start()
    for r in range(pieces):
        for copy in outof(r):
            copy.wait()


def unpack(event, raw, meta, inverse, shape, held):
    stripes, depth, stripe = shape
    half = ((depth // 2, stripe), jnp.bfloat16)
    pieces = 8
    given, aliases = [meta, inverse, raw], {}
    if held is not None:
        aliases[len(given)] = 0
        given.append(held)
    held, *halves = call(
        functools.partial(unpack_kernel, event),
        "unpack",
        given,
        1,
        [(shape, jnp.bfloat16), half, half],
        [
            pltpu.VMEM((depth, stripe), jnp.bfloat16),
            pltpu.VMEM((depth, stripe), jnp.bfloat16),
            pltpu.VMEM(inverse.shape, jnp.float32),
            pltpu.SemaphoreType.DMA((pieces,)),
            pltpu.SemaphoreType.DMA((2 * pieces,)),
            pltpu.SemaphoreType.DMA((pieces,)),
        ],
        aliases,
    )
    return held, halves


def dot(left, right):
    return lax.dot_general(left, right, (((0,), (0,)), ((), ())), preferred_element_type=jnp.float32)


def stage_kernel(cov_scale, stage, given, last, keeps, meta, lefts, rights, slots, spans, noise, *rest):
    given = rest[:given]
    inverse = given[1] if last else None
    held, out, lbuf, rbuf, scales, noises, outs, zeros, arrive, leave, streamed, noised, stored, fill = rest[-14:]
    _, height, stripe = out.shape
    depth = held.shape[1]
    rows = depth // 2
    ahead, behind = noises.shape[0], outs.shape[0]
    dead, here, begin, middle, end = spans[0], spans[1], *(spans[2 + 2 * stage + k] for k in range(3))
    place = meta[stage]
    columns = pl.ds(pl.multiple_of(here * height, height), height)
    sides = [pl.ds(h * rows, rows) for h in range(2)]
    sources = given or [held.at[place, side] for side in sides]
    if last:
        sources = [given[0].at[side] for side in sides]
    into = [pltpu.make_async_copy(sources[h], rbuf.at[0, sides[h]], arrive.at[h]) for h in range(2)]
    outof = [pltpu.make_async_copy(rbuf.at[0, side], held.at[place, side], leave.at[h]) for h, side in enumerate(sides)]

    def clear(e):
        return pltpu.make_async_copy(zeros, out.at[slots[e]], fill)

    def by_row(e):
        return e < middle

    def by_column(e):
        return (e >= middle) & (lefts[e] != rights[e])

    def fetch(e, step):
        b = lax.rem(e - begin, ahead)
        step(pltpu.make_async_copy(noise.at[slots[e]], noises.at[b], noised.at[b]))
        right = pltpu.make_async_copy(held.at[rights[e]], rbuf.at[1 + b], streamed.at[b])
        left = pltpu.make_async_copy(held.at[lefts[e], :, columns], lbuf.at[1 + b], streamed.at[b])
        pl.when(by_row(e))(lambda: step(right))
        pl.when(by_column(e))(lambda: step(left))

    def store(e):
        o = lax.rem(e - begin, behind)
        return pltpu.make_async_copy(outs.at[o], out.at[slots[e]], stored.at[o])

    def one_tile(e):
        b, o = lax.rem(e - begin, ahead), lax.rem(e - begin, behind)
        fetch(e, lambda copy: copy.wait())
        pl.when(e - begin >= behind)(lambda: store(e).wait())
        left = lbuf[jnp.where(by_column(e), 1 + b, 0)]
        right = rbuf[jnp.where(by_row(e), 1 + b, 0)]
        outs[o] = cov_scale * dot(left, right) + noises[b]
        store(e).start()
        pl.when(e + ahead < end)(lambda: fetch(e + ahead, lambda copy: copy.start()))

    if stage == CLEAR:

        @pl.when(dead > 0)
        def _():
            zeros[...] = jnp.zeros_like(zeros)
            pl.loop(0, dead)(lambda e: clear(e).start())

    @pl.when((end > begin) | keeps)
    def _():
        factors = pltpu.make_async_copy(inverse, scales, fill) if last else None
        if last:
            factors.start()
        for copy in into:
            copy.start()
        pl.loop(begin, jnp.minimum(begin + ahead, end))(lambda e: fetch(e, lambda copy: copy.start()))
        if last:
            factors.wait()
        for copy in into:
            copy.wait()
        if last:
            part = depth // 8

            @pl.loop(0, 8)
            def _(r):
                at = pl.ds(pl.multiple_of(r * part, part), part)
                rbuf[0, at] = (rbuf[0, at].astype(jnp.float32) * scales[at, :1]).astype(jnp.bfloat16)

        if keeps:
            for copy in outof:
                copy.start()

        @pl.when(end > begin)
        def _():
            lbuf[0] = rbuf[0, :, columns]
            pl.loop(begin, end)(one_tile)
            pl.loop(jnp.maximum(end - behind, begin), end)(lambda e: store(e).wait())

        if keeps:
            for copy in outof:
                copy.wait()

    if stage == CLEAR:
        pl.when(dead > 0)(lambda: pl.loop(0, dead)(lambda e: clear(e).wait()))


def run_stage(cov_scale, stage, arrays, meta, table, spans, noise, held, out):
    slots, height, stripe = noise.shape
    stripes, depth = held.shape[:2]
    final = 2 * len(EVENTS) - 1
    given = [meta, *table, spans, noise, *arrays, held]
    aliases = {len(given) - 1: 0}
    if out is not None:
        aliases[len(given)] = 1
        given.append(out)
    return call(
        functools.partial(stage_kernel, cov_scale, stage, len(arrays), stage >= final - 1, len(arrays) > 0 and stage < final),
        "stage",
        given,
        5,
        [(held.shape, jnp.bfloat16), (noise.shape, jnp.float32)],
        [
            pltpu.VMEM((1 + AHEAD, depth, height), jnp.bfloat16),
            pltpu.VMEM((1 + AHEAD, depth, stripe), jnp.bfloat16),
            pltpu.VMEM((depth, 128), jnp.float32),
            pltpu.VMEM((AHEAD, height, stripe), jnp.float32),
            pltpu.VMEM((BEHIND, height, stripe), jnp.float32),
            pltpu.VMEM((height, stripe), jnp.float32),
            pltpu.SemaphoreType.DMA((2,)),
            pltpu.SemaphoreType.DMA((2,)),
            pltpu.SemaphoreType.DMA((AHEAD,)),
            pltpu.SemaphoreType.DMA((AHEAD,)),
            pltpu.SemaphoreType.DMA((BEHIND,)),
            pltpu.SemaphoreType.DMA(()),
        ],
        aliases,
    )


def plain_kernel(cov_scale, lefts, rights, slots, spans, noise, held, out, zeros, fill):
    _, height, stripe = out.shape
    depth = held.shape[1]
    dead, here, end = spans[0], spans[1], spans[4]

    def clear(e):
        return pltpu.make_async_copy(zeros, out.at[slots[e]], fill)

    def one_tile(l, r, n, o):
        o[0] = cov_scale * dot(l[0], r[0]) + n[0]

    @pl.when(dead > 0)
    def _():
        zeros[...] = jnp.zeros_like(zeros)
        pl.loop(0, dead)(lambda e: clear(e).start())
        pl.loop(0, dead)(lambda e: clear(e).wait())

    tile = pl.BlockSpec((1, height, stripe), lambda e: (slots[dead + e], 0, 0))
    left = pl.BlockSpec((1, depth, height), lambda e: (lefts[dead + e], 0, here))
    right = pl.BlockSpec((1, depth, stripe), lambda e: (rights[dead + e], 0, 0))
    pl.when(end > dead)(
        lambda: pltpu.emit_pipeline(
            one_tile, grid=(end - dead,), in_specs=[left, right, tile], out_specs=[tile]
        )(held, held, noise, out)
    )


def schedule(first, second, living, stage_of, stages, core):
    slots = first.shape[0]
    look = lambda index: jnp.sum(
        jnp.where(index[:, None] == jnp.arange(stage_of.shape[0])[None, :], stage_of[None, :], 0), axis=1
    )
    one, two = look(first), look(second)
    stage = jnp.where(living > 0, 2 * jnp.maximum(one, two) + (two >= one).astype(jnp.int32), -1)
    position = jnp.arange(slots, dtype=jnp.int32)
    key = ((stage + 1) * 64 + second) * slots + position
    rank = jnp.sum((key[None, :] < key[:, None]).astype(jnp.int32), axis=1)
    pick = (rank[None, :] == position[:, None]).astype(jnp.int32)
    put = lambda values: jnp.sum(pick * values[None, :], axis=1)
    table = (put(first), put(second), put(position))
    bounds = jnp.sum((stage[None, :] < jnp.arange(2 * stages + 1)[:, None]).astype(jnp.int32), axis=1)
    return table, jnp.concatenate([bounds[:1], core.reshape(1), bounds]).astype(jnp.int32)


def grid_body(features, tile_lists, noise_tiles):
    slots, height, stripe = noise_tiles.shape
    rows = features.shape[0]
    chips = lax.axis_size("tile")
    stripes = features.shape[1] * chips // stripe
    shape = (stripes, 2 * rows, stripe)
    chip = lax.axis_index("tile")
    core = lax.axis_index("example").astype(jnp.int32)
    cov_scale = F / math.sqrt(rows * lax.axis_size("example"))
    slot = lambda k, x: lax.ppermute(x, ("tile", "example"), slot_pairs(k))
    swap = lambda x: lax.ppermute(x, "example", CORES)

    joint = lambda x, pairs: lax.ppermute(x, ("tile", "example"), pairs)
    place = core.reshape(1)

    mine = lax.dynamic_slice_in_dim(features, core * stripe, stripe, 1)
    first_mine = slot(0, mine)
    later, _ = lax.optimization_barrier((features, mine))
    other = swap(lax.dynamic_slice_in_dim(later, (1 - core) * stripe, stripe, 1))
    first_other = slot(0, other)

    values = later.astype(jnp.float32)
    squares = jnp.sum(values * values, axis=1)
    squares_other = swap(squares)
    both = jnp.where(core == 0, jnp.stack([squares, squares_other]), jnp.stack([squares_other, squares]))
    both = both + joint(both, [(2 * a, 2 * b) for a, b in Y_SWAP])
    both = jnp.where(core == 0, both, swap(both))
    norms = both
    for k in (1, 2, 3):
        source = lambda c: 2 * c + (0 if k > 1 and not is_end(c) else 1)
        norms = norms + joint(both, [(source(c), 2 * (c ^ (2 * k)) + 1) for c in range(chips)])
    raw = merge(place, mine, other)
    first_mine, first_other = keep([first_mine, first_other], [norms])
    [later] = keep([raw], [first_other])
    first_sent = merge(place, first_mine, first_other)
    norms = jnp.where(core == 1, norms, swap(norms)).reshape(2 * rows)
    inverse = 1.0 / jnp.maximum(jnp.sqrt(norms), math.sqrt(2.0 * F))
    inverse = jnp.broadcast_to(inverse[:, None], (2 * rows, 128))

    meta = lax.dynamic_index_in_dim(jnp.asarray(numbers(stripes)), 2 * chip + core, 0, keepdims=False)
    first, second, living = slot_table(tile_lists, chip, slots)
    table, spans = schedule(first, second, living, meta[2 * len(EVENTS) :], 2 * len(EVENTS), core)

    come = [first_sent, slot(1, later)]
    held = out = None
    for k, event in enumerate(EVENTS):
        raw = later if event == "own" else come[event]
        if event in (0, 2, 4):
            come.append(slot(event + 2, raw))
        if k < len(EVENTS) - 1:
            held, halves = unpack(k, raw, meta, inverse, shape, held)
            mine, theirs = [], [swap(x) for x in halves]
        else:
            [raw] = keep([raw], [out])
            mine, theirs = [raw, inverse], [swap(raw), inverse]
        held, out = run_stage(cov_scale, 2 * k, mine, meta, table, spans, noise_tiles, held, out)
        held, out = run_stage(cov_scale, 2 * k + 1, theirs, meta, table, spans, noise_tiles, held, out)
        if event in (1, 3):
            [come[event]] = keep([come[event]], [out])
            come.append(slot(event + 2, come[event]))
    return out


def plain_body(features, tile_lists, noise_tiles):
    slots, height, stripe = noise_tiles.shape
    rows = features.shape[0]
    chips = lax.axis_size("tile")
    stripes = features.shape[1] * chips // stripe
    core = lax.axis_index("example").astype(jnp.int32)
    cov_scale = F / math.sqrt(rows * lax.axis_size("example"))
    values = features.astype(jnp.float32)
    norms = lax.psum(jnp.sum(values * values, axis=1), "tile")
    inverse = (1.0 / jnp.maximum(jnp.sqrt(norms), math.sqrt(2.0 * F)))[:, None]
    scaled = (values * inverse).astype(jnp.bfloat16)
    wide = lax.all_gather(lax.all_gather(scaled, "tile", axis=1, tiled=True), "example", axis=0, tiled=True)
    held = wide.reshape(2 * rows, stripes, stripe).transpose(1, 0, 2)
    first, second, living = slot_table(tile_lists, lax.axis_index("tile"), slots)
    table, spans = schedule(first, second, living, jnp.zeros((stripes,), jnp.int32), 1, core)
    return call(
        functools.partial(plain_kernel, cov_scale),
        "plain",
        [*table, spans, noise_tiles, held],
        4,
        [(noise_tiles.shape, jnp.float32)],
        [pltpu.VMEM((height, stripe), jnp.float32), pltpu.SemaphoreType.DMA(())],
        {},
    )[0]


def body(features, tile_lists, noise_tiles):
    if lax.axis_size("tile") == 8 and features.shape[1] == 2 * noise_tiles.shape[2]:
        return grid_body(features, tile_lists, noise_tiles)
    return plain_body(features, tile_lists, noise_tiles)


def solution(mesh):
    placed = (
        P(("groups", "example"), "tile"),
        P("groups", None),
        P(("groups", "tile"), "example", None),
    )
    return jax.shard_map(
        body,
        mesh=mesh,
        in_specs=placed,
        out_specs=P(("groups", "tile"), "example", None),
        check_vma=False,
    )
```

```python
import functools
import math

import jax
import jax.numpy as jnp
import numpy as np
from jax import lax
from jax.experimental import pallas as pl
from jax.experimental.pallas import tpu as pltpu
from jax.sharding import PartitionSpec as P

F = 8192
VMEM = 63 * 1024 * 1024
CORES = [(0, 1), (1, 0)]

SLOTS = 7


def partner(chip, along):
    z, y = chip // 2, chip % 2
    if along == "y":
        return 2 * z + 1 - y
    return 2 * ((z ^ 1) if along == "z" else 3 - z) + y


def is_end(chip):
    return chip // 2 in (0, 3)


def z_core(k):
    return ((k + 1) // 2) % 2


def slot_pairs(k):
    c = z_core(k)
    pairs = []
    for chip in range(8):
        pairs.append((2 * chip + c, 2 * partner(chip, "z") + c))
        pairs.append((2 * chip + 1 - c, 2 * partner(chip, "y" if is_end(chip) else "m") + 1 - c))
    return pairs


Y_SWAP = [(chip, partner(chip, "y")) for chip in range(8)]


def slot_table(tile_lists, owner, slots):
    owners = tile_lists[:, 2]
    entries = tile_lists.shape[0]
    position = jnp.arange(entries, dtype=jnp.int32)
    mine = owners == owner
    earlier = (position[None, :] < position[:, None]) & mine[None, :]
    ranks = jnp.sum(earlier.astype(jnp.int32), axis=1)
    matches = (
        mine[None, :] & (ranks[None, :] == jnp.arange(slots, dtype=jnp.int32)[:, None])
    ).astype(jnp.int32)
    living = jnp.sum(matches, axis=1)
    first = jnp.sum(matches * tile_lists[None, :, 0], axis=1)
    second = jnp.sum(matches * tile_lists[None, :, 1], axis=1)
    return (first, second, living)


AHEAD, BEHIND, CLEAR = 6, 4, 4

EVENTS = ["own", 0, 1, 2, 3, 4, 5, 6]


def numbers(stripes):
    devices = range(16)
    got = {d: [] for d in devices}
    for k in range(SLOTS):
        sent = {d: (d if k < 2 else got[d][k - 2]) for d in devices}
        for a, b in slot_pairs(k):
            got[b].append(sent[a])
    table = np.zeros((16, 2 * len(EVENTS) + stripes), np.int32)
    for d in devices:
        row = table[d]
        places = row[2 * len(EVENTS) :]
        for k, event in enumerate(EVENTS):
            for j, who in enumerate((d, d ^ 1)):
                if event == "own":
                    stripe = who
                else:
                    stripe = got[who][event]
                row[2 * k + j] = stripe
                places[stripe] = 2 * k + j
        assert sorted(row[: 2 * len(EVENTS)]) == list(range(stripes))
    return table


def call(kernel, name, operands, scalars, results, scratch, aliases, after=(), space=pltpu.HBM):
    hbm = pl.BlockSpec(memory_space=space)
    operands = [*operands, *after]
    return pl.pallas_call(
        kernel,
        in_specs=[pl.BlockSpec(memory_space=pltpu.SMEM)] * scalars + [hbm] * (len(operands) - scalars),
        out_specs=[hbm] * len(results),
        out_shape=[jax.ShapeDtypeStruct(shape, dtype) for shape, dtype in results],
        scratch_shapes=scratch,
        input_output_aliases=aliases,
        compiler_params=pltpu.CompilerParams(vmem_limit_bytes=VMEM),
        cost_estimate=pl.CostEstimate(flops=1024, bytes_accessed=1024, transcendentals=0),
        name=name,
    )(*operands)


def keep(arrays, after):
    return call(
        lambda *_: None,
        "keep",
        arrays,
        0,
        [(x.shape, x.dtype) for x in arrays],
        [],
        {k: k for k in range(len(arrays))},
        after,
    )


def merge_kernel(place, mine, other, *rest):
    whole, room, arrive, leave = rest[-4:]
    core = place[0]
    rows, stripe = other.shape
    pieces = arrive.shape[0] // 2
    part = rows // pieces
    copies = []
    for k, (source, side) in enumerate(((mine, core), (other, 1 - core))):
        for r in range(pieces):
            at = pl.ds(r * part, part)
            target = pl.ds(pl.multiple_of(side * rows + r * part, part), part)
            spot = pieces * k + r
            copies.append((
                pltpu.make_async_copy(source.at[at], room.at[k, at], arrive.at[spot]),
                pltpu.make_async_copy(room.at[k, at], whole.at[target], leave.at[spot]),
            ))
    for into, _ in copies:
        into.start()
    for into, outof in copies:
        into.wait()
        outof.start()
    for _, outof in copies:
        outof.wait()


def merge(place, mine, other, after=()):
    rows, stripe = other.shape
    return call(
        merge_kernel,
        "merge",
        [place, mine, other],
        1,
        [((2 * rows, stripe), jnp.bfloat16)],
        [
            pltpu.VMEM((2, rows, stripe), jnp.bfloat16),
            pltpu.SemaphoreType.DMA((4,)),
            pltpu.SemaphoreType.DMA((4,)),
        ],
        {},
        after,
    )[0]


def unpack_kernel(event, whole, meta, inverse, raw, *rest):
    held, *halves = rest[-9 - whole : -6 - whole]
    taken, given, scales, arrive, leave, wide = rest[-6:]
    depth = held.shape[1]
    pieces = arrive.shape[0]
    part = depth // pieces
    place = meta[2 * event]

    def rows(r):
        return pl.ds(r * part, part)

    def into(r):
        return [
            pltpu.make_async_copy(raw.at[rows(r)], taken.at[rows(r)], arrive.at[r]),
            pltpu.make_async_copy(inverse.at[rows(r)], scales.at[rows(r)], wide.at[r]),
        ]

    def outof(r):
        half = pieces // 2
        copies = [
            pltpu.make_async_copy(given.at[rows(r)], halves[r // half].at[rows(r % half)], leave.at[3 * r]),
            pltpu.make_async_copy(given.at[rows(r)], held.at[place, rows(r)], leave.at[3 * r + 1]),
        ]
        if whole:
            copies.append(pltpu.make_async_copy(given.at[rows(r)], rest[-7].at[rows(r)], leave.at[3 * r + 2]))
        return copies

    for r in range(pieces):
        for copy in into(r):
            copy.start()
    for r in range(pieces):
        for copy in into(r):
            copy.wait()
        given[rows(r)] = (taken[rows(r)].astype(jnp.float32) * scales[rows(r), :1]).astype(jnp.bfloat16)
        for copy in outof(r):
            copy.start()
    for r in range(pieces):
        for copy in outof(r):
            copy.wait()


def unpack(event, whole, raw, meta, inverse, shape, held):
    stripes, depth, stripe = shape
    half = ((depth // 2, stripe), jnp.bfloat16)
    pieces = 8
    given, aliases = [meta, inverse, raw], {}
    if held is not None:
        aliases[len(given)] = 0
        given.append(held)
    held, *scaled = call(
        functools.partial(unpack_kernel, event, whole),
        "unpack",
        given,
        1,
        [(shape, jnp.bfloat16), half, half] + [((depth, stripe), jnp.bfloat16)] * whole,
        [
            pltpu.VMEM((depth, stripe), jnp.bfloat16),
            pltpu.VMEM((depth, stripe), jnp.bfloat16),
            pltpu.VMEM(inverse.shape, jnp.float32),
            pltpu.SemaphoreType.DMA((pieces,)),
            pltpu.SemaphoreType.DMA((3 * pieces,)),
            pltpu.SemaphoreType.DMA((pieces,)),
        ],
        aliases,
    )
    return held, scaled


def dot(left, right):
    return lax.dot_general(left, right, (((0,), (0,)), ((), ())), preferred_element_type=jnp.float32)


def stage_kernel(cov_scale, stage, given, last, keeps, meta, lefts, rights, slots, spans, noise, *rest):
    given = rest[:given]
    held, out, lbuf, rbuf, noises, outs, zeros, arrive, leave, streamed, noised, stored, fill = rest[-13:]
    _, height, stripe = out.shape
    depth = held.shape[1]
    rows = depth // 2
    ahead, behind = noises.shape[0], outs.shape[0]
    dead, here, begin, middle, end = spans[0], spans[1], *(spans[2 + 2 * stage + k] for k in range(3))
    place = meta[stage]
    columns = pl.ds(pl.multiple_of(here * height, height), height)
    sides = [pl.ds(h * rows, rows) for h in range(2)]
    sources = given or [held.at[place, side] for side in sides]
    if last:
        sources = [given[0].at[side] for side in sides]
    into = [pltpu.make_async_copy(sources[h], rbuf.at[0, sides[h]], arrive.at[h]) for h in range(2)]
    outof = [pltpu.make_async_copy(rbuf.at[0, side], held.at[place, side], leave.at[h]) for h, side in enumerate(sides)]

    def clear(e):
        return pltpu.make_async_copy(zeros, out.at[slots[e]], fill)

    def by_row(e):
        return e < middle

    def by_column(e):
        return (e >= middle) & (lefts[e] != rights[e])

    def fetch(e, step):
        b = lax.rem(e - begin, ahead)
        step(pltpu.make_async_copy(noise.at[slots[e]], noises.at[b], noised.at[b]))
        right = pltpu.make_async_copy(held.at[rights[e]], rbuf.at[1 + b], streamed.at[b])
        left = pltpu.make_async_copy(held.at[lefts[e], :, columns], lbuf.at[1 + b], streamed.at[b])
        pl.when(by_row(e))(lambda: step(right))
        pl.when(by_column(e))(lambda: step(left))

    def store(e):
        o = lax.rem(e - begin, behind)
        return pltpu.make_async_copy(outs.at[o], out.at[slots[e]], stored.at[o])

    def one_tile(e):
        b, o = lax.rem(e - begin, ahead), lax.rem(e - begin, behind)
        fetch(e, lambda copy: copy.wait())
        pl.when(e - begin >= behind)(lambda: store(e).wait())
        left = lbuf[jnp.where(by_column(e), 1 + b, 0)]
        right = rbuf[jnp.where(by_row(e), 1 + b, 0)]
        outs[o] = cov_scale * dot(left, right) + noises[b]
        store(e).start()
        pl.when(e + ahead < end)(lambda: fetch(e + ahead, lambda copy: copy.start()))

    if stage == CLEAR:

        @pl.when(dead > 0)
        def _():
            zeros[...] = jnp.zeros_like(zeros)
            pl.loop(0, dead)(lambda e: clear(e).start())

    @pl.when((end > begin) | keeps)
    def _():
        for copy in into:
            copy.start()
        pl.loop(begin, jnp.minimum(begin + ahead, end))(lambda e: fetch(e, lambda copy: copy.start()))
        for copy in into:
            copy.wait()
        if keeps:
            for copy in outof:
                copy.start()

        @pl.when(end > begin)
        def _():
            lbuf[0] = rbuf[0, :, columns]
            pl.loop(begin, end)(one_tile)
            pl.loop(jnp.maximum(end - behind, begin), end)(lambda e: store(e).wait())

        if keeps:
            for copy in outof:
                copy.wait()

    if stage == CLEAR:
        pl.when(dead > 0)(lambda: pl.loop(0, dead)(lambda e: clear(e).wait()))


def run_stage(cov_scale, stage, arrays, meta, table, spans, noise, held, out):
    slots, height, stripe = noise.shape
    stripes, depth = held.shape[:2]
    final = 2 * len(EVENTS) - 1
    given = [meta, *table, spans, noise, *arrays, held]
    aliases = {len(given) - 1: 0}
    if out is not None:
        aliases[len(given)] = 1
        given.append(out)
    return call(
        functools.partial(stage_kernel, cov_scale, stage, len(arrays), stage >= final - 1, len(arrays) > 0 and stage < final),
        "stage",
        given,
        5,
        [(held.shape, jnp.bfloat16), (noise.shape, jnp.float32)],
        [
            pltpu.VMEM((1 + AHEAD, depth, height), jnp.bfloat16),
            pltpu.VMEM((1 + AHEAD, depth, stripe), jnp.bfloat16),
            pltpu.VMEM((AHEAD, height, stripe), jnp.float32),
            pltpu.VMEM((BEHIND, height, stripe), jnp.float32),
            pltpu.VMEM((height, stripe), jnp.float32),
            pltpu.SemaphoreType.DMA((2,)),
            pltpu.SemaphoreType.DMA((2,)),
            pltpu.SemaphoreType.DMA((AHEAD,)),
            pltpu.SemaphoreType.DMA((AHEAD,)),
            pltpu.SemaphoreType.DMA((BEHIND,)),
            pltpu.SemaphoreType.DMA(()),
        ],
        aliases,
    )


def plain_kernel(cov_scale, lefts, rights, slots, spans, noise, held, out, zeros, fill):
    _, height, stripe = out.shape
    depth = held.shape[1]
    dead, here, end = spans[0], spans[1], spans[4]

    def clear(e):
        return pltpu.make_async_copy(zeros, out.at[slots[e]], fill)

    def one_tile(l, r, n, o):
        o[0] = cov_scale * dot(l[0], r[0]) + n[0]

    @pl.when(dead > 0)
    def _():
        zeros[...] = jnp.zeros_like(zeros)
        pl.loop(0, dead)(lambda e: clear(e).start())
        pl.loop(0, dead)(lambda e: clear(e).wait())

    tile = pl.BlockSpec((1, height, stripe), lambda e: (slots[dead + e], 0, 0))
    left = pl.BlockSpec((1, depth, height), lambda e: (lefts[dead + e], 0, here))
    right = pl.BlockSpec((1, depth, stripe), lambda e: (rights[dead + e], 0, 0))
    pl.when(end > dead)(
        lambda: pltpu.emit_pipeline(
            one_tile, grid=(end - dead,), in_specs=[left, right, tile], out_specs=[tile]
        )(held, held, noise, out)
    )


def schedule(first, second, living, stage_of, stages, core):
    slots = first.shape[0]
    look = lambda index: jnp.sum(
        jnp.where(index[:, None] == jnp.arange(stage_of.shape[0])[None, :], stage_of[None, :], 0), axis=1
    )
    one, two = look(first), look(second)
    stage = jnp.where(living > 0, 2 * jnp.maximum(one, two) + (two >= one).astype(jnp.int32), -1)
    position = jnp.arange(slots, dtype=jnp.int32)
    key = ((stage + 1) * 64 + second) * slots + position
    rank = jnp.sum((key[None, :] < key[:, None]).astype(jnp.int32), axis=1)
    pick = (rank[None, :] == position[:, None]).astype(jnp.int32)
    put = lambda values: jnp.sum(pick * values[None, :], axis=1)
    table = (put(first), put(second), put(position))
    bounds = jnp.sum((stage[None, :] < jnp.arange(2 * stages + 1)[:, None]).astype(jnp.int32), axis=1)
    return table, jnp.concatenate([bounds[:1], core.reshape(1), bounds]).astype(jnp.int32)


def grid_body(features, tile_lists, noise_tiles):
    slots, height, stripe = noise_tiles.shape
    rows = features.shape[0]
    chips = lax.axis_size("tile")
    stripes = features.shape[1] * chips // stripe
    shape = (stripes, 2 * rows, stripe)
    chip = lax.axis_index("tile")
    core = lax.axis_index("example").astype(jnp.int32)
    cov_scale = F / math.sqrt(rows * lax.axis_size("example"))
    slot = lambda k, x: lax.ppermute(x, ("tile", "example"), slot_pairs(k))
    swap = lambda x: lax.ppermute(x, "example", CORES)

    joint = lambda x, pairs: lax.ppermute(x, ("tile", "example"), pairs)
    place = core.reshape(1)

    mine = lax.dynamic_slice_in_dim(features, core * stripe, stripe, 1)
    first_mine = slot(0, mine)
    later, _ = lax.optimization_barrier((features, mine))
    other = swap(lax.dynamic_slice_in_dim(later, (1 - core) * stripe, stripe, 1))
    first_other = slot(0, other)

    values = later.astype(jnp.float32)
    squares = jnp.sum(values * values, axis=1)
    squares_other = swap(squares)
    both = jnp.where(core == 0, jnp.stack([squares, squares_other]), jnp.stack([squares_other, squares]))
    both = both + joint(both, [(2 * a, 2 * b) for a, b in Y_SWAP])
    both = jnp.where(core == 0, both, swap(both))
    last, first_mine = keep([both, first_mine], [])
    norms = both
    for k in (1, 2, 3):
        source = lambda c: 2 * c + (0 if k > 1 and not is_end(c) else 1)
        message = both if k < 3 else last
        norms = norms + joint(message, [(source(c), 2 * (c ^ (2 * k)) + 1) for c in range(chips)])
    raw = merge(place, mine, other)
    [first_other] = keep([first_other], [norms])
    [later] = keep([raw], [first_other])
    first_sent = merge(place, first_mine, first_other)
    norms = jnp.where(core == 1, norms, swap(norms)).reshape(2 * rows)
    inverse = 1.0 / jnp.maximum(jnp.sqrt(norms), math.sqrt(2.0 * F))
    inverse = jnp.broadcast_to(inverse[:, None], (2 * rows, 128))

    meta = lax.dynamic_index_in_dim(jnp.asarray(numbers(stripes)), 2 * chip + core, 0, keepdims=False)
    first, second, living = slot_table(tile_lists, chip, slots)
    table, spans = schedule(first, second, living, meta[2 * len(EVENTS) :], 2 * len(EVENTS), core)

    come = [first_sent, slot(1, later)]
    held = out = None
    for k, event in enumerate(EVENTS):
        raw = later if event == "own" else come[event]
        if event in (0, 2):
            come.append(slot(event + 2, raw))
        if k < len(EVENTS) - 1:
            held, scaled = unpack(k, event == 4, raw, meta, inverse, shape, held)
            mine, theirs = [], [swap(x) for x in scaled[:2]]
            if event == 4:
                come.append(slot(6, scaled[2]))
        else:
            [raw] = keep([raw], [out])
            mine, theirs = [raw], [swap(raw)]
        held, out = run_stage(cov_scale, 2 * k, mine, meta, table, spans, noise_tiles, held, out)
        if event == 1:
            [come[1]] = keep([come[1]], [out])
            come.append(slot(3, come[1]))
        held, out = run_stage(cov_scale, 2 * k + 1, theirs, meta, table, spans, noise_tiles, held, out)
        if event == 3:
            [come[3]] = keep([come[3]], [out])
            come.append(slot(5, come[3]))
    return out


def plain_body(features, tile_lists, noise_tiles):
    slots, height, stripe = noise_tiles.shape
    rows = features.shape[0]
    chips = lax.axis_size("tile")
    stripes = features.shape[1] * chips // stripe
    core = lax.axis_index("example").astype(jnp.int32)
    cov_scale = F / math.sqrt(rows * lax.axis_size("example"))
    values = features.astype(jnp.float32)
    norms = lax.psum(jnp.sum(values * values, axis=1), "tile")
    inverse = (1.0 / jnp.maximum(jnp.sqrt(norms), math.sqrt(2.0 * F)))[:, None]
    scaled = (values * inverse).astype(jnp.bfloat16)
    wide = lax.all_gather(lax.all_gather(scaled, "tile", axis=1, tiled=True), "example", axis=0, tiled=True)
    held = wide.reshape(2 * rows, stripes, stripe).transpose(1, 0, 2)
    first, second, living = slot_table(tile_lists, lax.axis_index("tile"), slots)
    table, spans = schedule(first, second, living, jnp.zeros((stripes,), jnp.int32), 1, core)
    return call(
        functools.partial(plain_kernel, cov_scale),
        "plain",
        [*table, spans, noise_tiles, held],
        4,
        [(noise_tiles.shape, jnp.float32)],
        [pltpu.VMEM((height, stripe), jnp.float32), pltpu.SemaphoreType.DMA(())],
        {},
    )[0]


def body(features, tile_lists, noise_tiles):
    if lax.axis_size("tile") == 8 and features.shape[1] == 2 * noise_tiles.shape[2]:
        return grid_body(features, tile_lists, noise_tiles)
    return plain_body(features, tile_lists, noise_tiles)


def solution(mesh):
    placed = (
        P(("groups", "example"), "tile"),
        P("groups", None),
        P(("groups", "tile"), "example", None),
    )
    return jax.shard_map(
        body,
        mesh=mesh,
        in_specs=placed,
        out_specs=P(("groups", "tile"), "example", None),
        check_vma=False,
    )
```

```python
import functools
import math

import jax
import jax.numpy as jnp
import numpy as np
from jax import lax
from jax.experimental import pallas as pl
from jax.experimental.pallas import tpu as pltpu
from jax.sharding import PartitionSpec as P

F = 8192
VMEM = 63 * 1024 * 1024
CORES = [(0, 1), (1, 0)]

SLOTS = 7


def partner(chip, along):
    z, y = chip // 2, chip % 2
    if along == "y":
        return 2 * z + 1 - y
    return 2 * ((z ^ 1) if along == "z" else 3 - z) + y


def is_end(chip):
    return chip // 2 in (0, 3)


def z_core(k):
    return ((k + 1) // 2) % 2


def slot_pairs(k):
    c = z_core(k)
    pairs = []
    for chip in range(8):
        pairs.append((2 * chip + c, 2 * partner(chip, "z") + c))
        pairs.append((2 * chip + 1 - c, 2 * partner(chip, "y" if is_end(chip) else "m") + 1 - c))
    return pairs


Y_SWAP = [(chip, partner(chip, "y")) for chip in range(8)]


def slot_table(tile_lists, owner, slots):
    owners = tile_lists[:, 2]
    entries = tile_lists.shape[0]
    position = jnp.arange(entries, dtype=jnp.int32)
    mine = owners == owner
    earlier = (position[None, :] < position[:, None]) & mine[None, :]
    ranks = jnp.sum(earlier.astype(jnp.int32), axis=1)
    matches = (
        mine[None, :] & (ranks[None, :] == jnp.arange(slots, dtype=jnp.int32)[:, None])
    ).astype(jnp.int32)
    living = jnp.sum(matches, axis=1)
    first = jnp.sum(matches * tile_lists[None, :, 0], axis=1)
    second = jnp.sum(matches * tile_lists[None, :, 1], axis=1)
    return (first, second, living)


AHEAD, BEHIND, CLEAR = 6, 4, 4

EVENTS = ["own", 0, 1, 2, 3, 4, 5, 6]


def numbers(stripes):
    devices = range(16)
    got = {d: [] for d in devices}
    for k in range(SLOTS):
        sent = {d: (d if k < 2 else got[d][k - 2]) for d in devices}
        for a, b in slot_pairs(k):
            got[b].append(sent[a])
    table = np.zeros((16, 2 * len(EVENTS) + stripes), np.int32)
    for d in devices:
        row = table[d]
        places = row[2 * len(EVENTS) :]
        for k, event in enumerate(EVENTS):
            for j, who in enumerate((d, d ^ 1)):
                if event == "own":
                    stripe = who
                else:
                    stripe = got[who][event]
                row[2 * k + j] = stripe
                places[stripe] = 2 * k + j
        assert sorted(row[: 2 * len(EVENTS)]) == list(range(stripes))
    return table


def call(kernel, name, operands, scalars, results, scratch, aliases, after=(), space=pltpu.HBM):
    hbm = pl.BlockSpec(memory_space=space)
    operands = [*operands, *after]
    return pl.pallas_call(
        kernel,
        in_specs=[pl.BlockSpec(memory_space=pltpu.SMEM)] * scalars + [hbm] * (len(operands) - scalars),
        out_specs=[hbm] * len(results),
        out_shape=[jax.ShapeDtypeStruct(shape, dtype) for shape, dtype in results],
        scratch_shapes=scratch,
        input_output_aliases=aliases,
        compiler_params=pltpu.CompilerParams(vmem_limit_bytes=VMEM),
        cost_estimate=pl.CostEstimate(flops=1024, bytes_accessed=1024, transcendentals=0),
        name=name,
    )(*operands)


def keep(arrays, after):
    return call(
        lambda *_: None,
        "keep",
        arrays,
        0,
        [(x.shape, x.dtype) for x in arrays],
        [],
        {k: k for k in range(len(arrays))},
        after,
    )


def merge_kernel(place, mine, other, *rest):
    whole, room, arrive, leave = rest[-4:]
    core = place[0]
    rows, stripe = other.shape
    pieces = arrive.shape[0] // 2
    part = rows // pieces
    copies = []
    for k, (source, side) in enumerate(((mine, core), (other, 1 - core))):
        for r in range(pieces):
            at = pl.ds(r * part, part)
            target = pl.ds(pl.multiple_of(side * rows + r * part, part), part)
            spot = pieces * k + r
            copies.append((
                pltpu.make_async_copy(source.at[at], room.at[k, at], arrive.at[spot]),
                pltpu.make_async_copy(room.at[k, at], whole.at[target], leave.at[spot]),
            ))
    for into, _ in copies:
        into.start()
    for into, outof in copies:
        into.wait()
        outof.start()
    for _, outof in copies:
        outof.wait()


def merge(place, mine, other, after=()):
    rows, stripe = other.shape
    return call(
        merge_kernel,
        "merge",
        [place, mine, other],
        1,
        [((2 * rows, stripe), jnp.bfloat16)],
        [
            pltpu.VMEM((2, rows, stripe), jnp.bfloat16),
            pltpu.SemaphoreType.DMA((4,)),
            pltpu.SemaphoreType.DMA((4,)),
        ],
        {},
        after,
    )[0]


def unpack_kernel(event, whole, meta, inverse, raw, *rest):
    held, *halves = rest[-9 - whole : -6 - whole]
    taken, given, scales, arrive, leave, wide = rest[-6:]
    depth = held.shape[1]
    pieces = arrive.shape[0]
    part = depth // pieces
    place = meta[2 * event]

    def rows(r):
        return pl.ds(r * part, part)

    def into(r):
        return [
            pltpu.make_async_copy(raw.at[rows(r)], taken.at[rows(r)], arrive.at[r]),
            pltpu.make_async_copy(inverse.at[rows(r)], scales.at[rows(r)], wide.at[r]),
        ]

    def outof(r):
        half = pieces // 2
        copies = [
            pltpu.make_async_copy(given.at[rows(r)], halves[r // half].at[rows(r % half)], leave.at[3 * r]),
            pltpu.make_async_copy(given.at[rows(r)], held.at[place, rows(r)], leave.at[3 * r + 1]),
        ]
        if whole:
            copies.append(pltpu.make_async_copy(given.at[rows(r)], rest[-7].at[rows(r)], leave.at[3 * r + 2]))
        return copies

    for r in range(pieces):
        for copy in into(r):
            copy.start()
    for r in range(pieces):
        for copy in into(r):
            copy.wait()
        given[rows(r)] = (taken[rows(r)].astype(jnp.float32) * scales[rows(r), :1]).astype(jnp.bfloat16)
        for copy in outof(r):
            copy.start()
    for r in range(pieces):
        for copy in outof(r):
            copy.wait()


def unpack(event, whole, raw, meta, inverse, shape, held):
    stripes, depth, stripe = shape
    half = ((depth // 2, stripe), jnp.bfloat16)
    pieces = 8
    given, aliases = [meta, inverse, raw], {}
    if held is not None:
        aliases[len(given)] = 0
        given.append(held)
    held, *scaled = call(
        functools.partial(unpack_kernel, event, whole),
        "unpack",
        given,
        1,
        [(shape, jnp.bfloat16), half, half] + [((depth, stripe), jnp.bfloat16)] * whole,
        [
            pltpu.VMEM((depth, stripe), jnp.bfloat16),
            pltpu.VMEM((depth, stripe), jnp.bfloat16),
            pltpu.VMEM(inverse.shape, jnp.float32),
            pltpu.SemaphoreType.DMA((pieces,)),
            pltpu.SemaphoreType.DMA((3 * pieces,)),
            pltpu.SemaphoreType.DMA((pieces,)),
        ],
        aliases,
    )
    return held, scaled


def dot(left, right):
    return lax.dot_general(left, right, (((0,), (0,)), ((), ())), preferred_element_type=jnp.float32)


def stage_kernel(cov_scale, stage, given, last, keeps, meta, lefts, rights, slots, spans, noise, *rest):
    given = rest[:given]
    held, out, lbuf, rbuf, noises, outs, zeros, arrive, leave, streamed, noised, stored, fill = rest[-13:]
    _, height, stripe = out.shape
    depth = held.shape[1]
    rows = depth // 2
    ahead, behind = noises.shape[0], outs.shape[0]
    dead, here, begin, middle, end = spans[0], spans[1], *(spans[2 + 2 * stage + k] for k in range(3))
    place = meta[stage]
    columns = pl.ds(pl.multiple_of(here * height, height), height)
    sides = [pl.ds(h * rows, rows) for h in range(2)]
    sources = given or [held.at[place, side] for side in sides]
    if last:
        sources = [given[0].at[side] for side in sides]
    into = [pltpu.make_async_copy(sources[h], rbuf.at[0, sides[h]], arrive.at[h]) for h in range(2)]
    outof = [pltpu.make_async_copy(rbuf.at[0, side], held.at[place, side], leave.at[h]) for h, side in enumerate(sides)]

    def clear(e):
        return pltpu.make_async_copy(zeros, out.at[slots[e]], fill)

    def by_row(e):
        return e < middle

    def by_column(e):
        return (e >= middle) & (lefts[e] != rights[e])

    def fetch(e, step):
        b = lax.rem(e - begin, ahead)
        step(pltpu.make_async_copy(noise.at[slots[e]], noises.at[b], noised.at[b]))
        right = pltpu.make_async_copy(held.at[rights[e]], rbuf.at[1 + b], streamed.at[b])
        left = pltpu.make_async_copy(held.at[lefts[e], :, columns], lbuf.at[1 + b], streamed.at[b])
        pl.when(by_row(e))(lambda: step(right))
        pl.when(by_column(e))(lambda: step(left))

    def store(e):
        o = lax.rem(e - begin, behind)
        return pltpu.make_async_copy(outs.at[o], out.at[slots[e]], stored.at[o])

    def one_tile(e):
        b, o = lax.rem(e - begin, ahead), lax.rem(e - begin, behind)
        fetch(e, lambda copy: copy.wait())
        pl.when(e - begin >= behind)(lambda: store(e).wait())
        left = lbuf[jnp.where(by_column(e), 1 + b, 0)]
        right = rbuf[jnp.where(by_row(e), 1 + b, 0)]
        outs[o] = cov_scale * dot(left, right) + noises[b]
        store(e).start()
        pl.when(e + ahead < end)(lambda: fetch(e + ahead, lambda copy: copy.start()))

    if stage == CLEAR:

        @pl.when(dead > 0)
        def _():
            zeros[...] = jnp.zeros_like(zeros)
            pl.loop(0, dead)(lambda e: clear(e).start())

    @pl.when((end > begin) | keeps)
    def _():
        for copy in into:
            copy.start()
        pl.loop(begin, jnp.minimum(begin + ahead, end))(lambda e: fetch(e, lambda copy: copy.start()))
        for copy in into:
            copy.wait()
        if keeps:
            for copy in outof:
                copy.start()

        @pl.when(end > begin)
        def _():
            lbuf[0] = rbuf[0, :, columns]
            pl.loop(begin, end)(one_tile)
            pl.loop(jnp.maximum(end - behind, begin), end)(lambda e: store(e).wait())

        if keeps:
            for copy in outof:
                copy.wait()

    if stage == CLEAR:
        pl.when(dead > 0)(lambda: pl.loop(0, dead)(lambda e: clear(e).wait()))


def run_stage(cov_scale, stage, arrays, meta, table, spans, noise, held, out):
    slots, height, stripe = noise.shape
    stripes, depth = held.shape[:2]
    final = 2 * len(EVENTS) - 1
    given = [meta, *table, spans, noise, *arrays, held]
    aliases = {len(given) - 1: 0}
    if out is not None:
        aliases[len(given)] = 1
        given.append(out)
    return call(
        functools.partial(stage_kernel, cov_scale, stage, len(arrays), stage >= final - 1, len(arrays) > 0 and stage < final),
        "stage",
        given,
        5,
        [(held.shape, jnp.bfloat16), (noise.shape, jnp.float32)],
        [
            pltpu.VMEM((1 + AHEAD, depth, height), jnp.bfloat16),
            pltpu.VMEM((1 + AHEAD, depth, stripe), jnp.bfloat16),
            pltpu.VMEM((AHEAD, height, stripe), jnp.float32),
            pltpu.VMEM((BEHIND, height, stripe), jnp.float32),
            pltpu.VMEM((height, stripe), jnp.float32),
            pltpu.SemaphoreType.DMA((2,)),
            pltpu.SemaphoreType.DMA((2,)),
            pltpu.SemaphoreType.DMA((AHEAD,)),
            pltpu.SemaphoreType.DMA((AHEAD,)),
            pltpu.SemaphoreType.DMA((BEHIND,)),
            pltpu.SemaphoreType.DMA(()),
        ],
        aliases,
    )


def plain_kernel(cov_scale, lefts, rights, slots, spans, noise, held, out, zeros, fill):
    _, height, stripe = out.shape
    depth = held.shape[1]
    dead, here, end = spans[0], spans[1], spans[4]

    def clear(e):
        return pltpu.make_async_copy(zeros, out.at[slots[e]], fill)

    def one_tile(l, r, n, o):
        o[0] = cov_scale * dot(l[0], r[0]) + n[0]

    @pl.when(dead > 0)
    def _():
        zeros[...] = jnp.zeros_like(zeros)
        pl.loop(0, dead)(lambda e: clear(e).start())
        pl.loop(0, dead)(lambda e: clear(e).wait())

    tile = pl.BlockSpec((1, height, stripe), lambda e: (slots[dead + e], 0, 0))
    left = pl.BlockSpec((1, depth, height), lambda e: (lefts[dead + e], 0, here))
    right = pl.BlockSpec((1, depth, stripe), lambda e: (rights[dead + e], 0, 0))
    pl.when(end > dead)(
        lambda: pltpu.emit_pipeline(
            one_tile, grid=(end - dead,), in_specs=[left, right, tile], out_specs=[tile]
        )(held, held, noise, out)
    )


def schedule(first, second, living, stage_of, stages, core):
    slots = first.shape[0]
    look = lambda index: jnp.sum(
        jnp.where(index[:, None] == jnp.arange(stage_of.shape[0])[None, :], stage_of[None, :], 0), axis=1
    )
    one, two = look(first), look(second)
    stage = jnp.where(living > 0, 2 * jnp.maximum(one, two) + (two >= one).astype(jnp.int32), -1)
    position = jnp.arange(slots, dtype=jnp.int32)
    key = ((stage + 1) * 64 + second) * slots + position
    rank = jnp.sum((key[None, :] < key[:, None]).astype(jnp.int32), axis=1)
    pick = (rank[None, :] == position[:, None]).astype(jnp.int32)
    put = lambda values: jnp.sum(pick * values[None, :], axis=1)
    table = (put(first), put(second), put(position))
    bounds = jnp.sum((stage[None, :] < jnp.arange(2 * stages + 1)[:, None]).astype(jnp.int32), axis=1)
    return table, jnp.concatenate([bounds[:1], core.reshape(1), bounds]).astype(jnp.int32)


def grid_body(features, tile_lists, noise_tiles):
    slots, height, stripe = noise_tiles.shape
    rows = features.shape[0]
    chips = lax.axis_size("tile")
    stripes = features.shape[1] * chips // stripe
    shape = (stripes, 2 * rows, stripe)
    chip = lax.axis_index("tile")
    core = lax.axis_index("example").astype(jnp.int32)
    cov_scale = F / math.sqrt(rows * lax.axis_size("example"))
    slot = lambda k, x: lax.ppermute(x, ("tile", "example"), slot_pairs(k))
    swap = lambda x: lax.ppermute(x, "example", CORES)

    joint = lambda x, pairs: lax.ppermute(x, ("tile", "example"), pairs)
    place = core.reshape(1)

    mine = lax.dynamic_slice_in_dim(features, core * stripe, stripe, 1)
    first_mine = slot(0, mine)
    later, _ = lax.optimization_barrier((features, mine))
    other = swap(lax.dynamic_slice_in_dim(later, (1 - core) * stripe, stripe, 1))
    first_other = slot(0, other)

    values = later.astype(jnp.float32)
    squares = jnp.sum(values * values, axis=1)
    squares_other = swap(squares)
    both = jnp.where(core == 0, jnp.stack([squares, squares_other]), jnp.stack([squares_other, squares]))
    both = both + joint(both, [(2 * a, 2 * b) for a, b in Y_SWAP])
    both = jnp.where(core == 0, both, swap(both))
    last, first_mine = keep([both, first_mine], [])
    norms = both
    for k in (1, 2, 3):
        source = lambda c: 2 * c + (0 if k > 1 and not is_end(c) else 1)
        message = both if k < 3 else last
        norms = norms + joint(message, [(source(c), 2 * (c ^ (2 * k)) + 1) for c in range(chips)])
    raw = merge(place, mine, other)
    [first_other] = keep([first_other], [norms])
    [later] = keep([raw], [first_other])
    [norms] = keep([norms], [later])
    first_sent = merge(place, first_mine, first_other)
    norms = jnp.where(core == 1, norms, swap(norms)).reshape(2 * rows)
    inverse = 1.0 / jnp.maximum(jnp.sqrt(norms), math.sqrt(2.0 * F))
    inverse = jnp.broadcast_to(inverse[:, None], (2 * rows, 128))

    meta = lax.dynamic_index_in_dim(jnp.asarray(numbers(stripes)), 2 * chip + core, 0, keepdims=False)
    first, second, living = slot_table(tile_lists, chip, slots)
    table, spans = schedule(first, second, living, meta[2 * len(EVENTS) :], 2 * len(EVENTS), core)

    come = [first_sent, slot(1, later)]
    held = out = None
    for k, event in enumerate(EVENTS):
        raw = later if event == "own" else come[event]
        if event in (0, 2):
            come.append(slot(event + 2, raw))
        if k < len(EVENTS) - 1:
            held, scaled = unpack(k, event == 4, raw, meta, inverse, shape, held)
            mine, theirs = [], [swap(x) for x in scaled[:2]]
            if event == 4:
                come.append(slot(6, scaled[2]))
        else:
            [raw] = keep([raw], [out])
            mine, theirs = [raw], [swap(raw)]
        held, out = run_stage(cov_scale, 2 * k, mine, meta, table, spans, noise_tiles, held, out)
        if event == 1:
            [come[1]] = keep([come[1]], [out])
            come.append(slot(3, come[1]))
        held, out = run_stage(cov_scale, 2 * k + 1, theirs, meta, table, spans, noise_tiles, held, out)
        if event == 3:
            [come[3]] = keep([come[3]], [out])
            come.append(slot(5, come[3]))
    return out


def plain_body(features, tile_lists, noise_tiles):
    slots, height, stripe = noise_tiles.shape
    rows = features.shape[0]
    chips = lax.axis_size("tile")
    stripes = features.shape[1] * chips // stripe
    core = lax.axis_index("example").astype(jnp.int32)
    cov_scale = F / math.sqrt(rows * lax.axis_size("example"))
    values = features.astype(jnp.float32)
    norms = lax.psum(jnp.sum(values * values, axis=1), "tile")
    inverse = (1.0 / jnp.maximum(jnp.sqrt(norms), math.sqrt(2.0 * F)))[:, None]
    scaled = (values * inverse).astype(jnp.bfloat16)
    wide = lax.all_gather(lax.all_gather(scaled, "tile", axis=1, tiled=True), "example", axis=0, tiled=True)
    held = wide.reshape(2 * rows, stripes, stripe).transpose(1, 0, 2)
    first, second, living = slot_table(tile_lists, lax.axis_index("tile"), slots)
    table, spans = schedule(first, second, living, jnp.zeros((stripes,), jnp.int32), 1, core)
    return call(
        functools.partial(plain_kernel, cov_scale),
        "plain",
        [*table, spans, noise_tiles, held],
        4,
        [(noise_tiles.shape, jnp.float32)],
        [pltpu.VMEM((height, stripe), jnp.float32), pltpu.SemaphoreType.DMA(())],
        {},
    )[0]


def body(features, tile_lists, noise_tiles):
    if lax.axis_size("tile") == 8 and features.shape[1] == 2 * noise_tiles.shape[2]:
        return grid_body(features, tile_lists, noise_tiles)
    return plain_body(features, tile_lists, noise_tiles)


def solution(mesh):
    placed = (
        P(("groups", "example"), "tile"),
        P("groups", None),
        P(("groups", "tile"), "example", None),
    )
    return jax.shard_map(
        body,
        mesh=mesh,
        in_specs=placed,
        out_specs=P(("groups", "tile"), "example", None),
        check_vma=False,
    )
```
